256 devices in a mesh: inst: 32 (over x, z_hi, core), tp: 8 (over z_lo, y).
Axes of the slice: x: 4, y: 4, z: 8 (z_hi: 4, z_lo: 2; z = z_hi * 2 + z_lo), core: 2. Of those that a mesh axis runs over, the one named last changes fastest.
Arguments:
- new_states: bfloat16 [3, 1024, 4096], P(None, 'inst'), may hold values from -6 to 6
- attn_gain: bfloat16 [4096], replicated, may hold values from 0.099609375 to 1.8984375
- q_weight: bfloat16 [4096, 4096], P(None, 'tp'), may hold values from -0.09375 to 0.09375
- k_weight: bfloat16 [4096, 1024], P(None, 'tp'), may hold values from -0.1875 to 0.1875
- v_weight: bfloat16 [4096, 1024], P(None, 'tp'), may hold values from -0.09375 to 0.09375
- o_weight: bfloat16 [4096, 4096], P('tp'), may hold values from -0.5 to 0.5
- prompt_keys: bfloat16 [32, 2048, 1024], P('inst', None, 'tp'), may hold values from -100 to 100
- prompt_values: bfloat16 [32, 2048, 1024], P('inst', None, 'tp'), may hold values from -6 to 6
- owner_index: int32 [1], replicated, may hold values from 0 to 31
Outputs:
- branch_out: bfloat16 [3, 1024, 4096], P(None, 'inst')
The draws below stay inside these ranges and needn't reach their ends.
All inputs are finite; a program needn't handle non-finite values.
Results may differ from the reference program's by a relative error of at most 0.019.
The reference program's roundings to bfloat16 on the way count: a program that leaves them out, or rounds other values in their place, can miss the bound.
Values may be sent and summed in bfloat16 or wider, within the bound.
No kernel may reach another device: no remote copies, remote signals or barrier semaphores. Data moves between devices by JAX's collectives and lax.ppermute only.
A program may use at most 64 MiB of HBM per device.

```python
import jax
import jax.numpy as jnp
from jax import lax

D = 4096
HD = 128
QPK = 4
STEPS = 3
PROMPT = 2048
KVH = 8
SAMPLES = 1024
N_INST = 32


def draw_prompt_keys(key, part):
    key = jax.random.fold_in(key, 11)
    shape = (N_INST, PROMPT, KVH * HD)
    base_key = jax.random.fold_in(key, 0)
    values = jnp.clip(2.0 * jax.random.normal(base_key, shape, jnp.float32), -8.0, 8.0)
    return values.astype(jnp.bfloat16)


def block_levels(own_key, shape, cuts, low, high):
    loudness = 1.0
    for axis_at, shards_of in cuts:
        draws = jax.random.uniform(jax.random.fold_in(jax.random.fold_in(own_key, 6), axis_at), (shards_of,), jnp.float32, low / len(cuts), high / len(cuts))
        loudness = loudness * jnp.repeat(jnp.exp(draws), shape[axis_at] // shards_of).reshape((-1,) + (1,) * (len(shape) - 1 - axis_at))
    return loudness


def bell_draw(own_key, dims, width, reach, pieces=(), held_as=jnp.bfloat16):
    values = jax.random.normal(own_key, dims, jnp.float32) * width
    if len(pieces) > 0:
        values = block_levels(own_key, dims, pieces, -0.22, 0.18) * values
    return jnp.clip(values, min=-reach, max=reach).astype(held_as)


def setup_inputs(seed: int = 0) -> dict:
    keys = jax.random.split(jax.random.key(seed), 10)
    return {
        "new_states": bell_draw(keys[0], (STEPS, SAMPLES, D), 1.0, 6.0, ((1, 32),)),
        "attn_gain": jnp.clip(1.0 + 0.18 * jax.random.normal(keys[1], (D,), jnp.float32), 0.099609375, 1.8984375).astype(jnp.bfloat16),
        "q_weight": bell_draw(keys[2], (D, KVH * QPK * HD), D ** -0.5, 0.09375, ((1, 8),)),
        "k_weight": bell_draw(keys[3], (D, KVH * HD), (D // 4) ** -0.5, 0.1875, ((1, 8),)),
        "v_weight": bell_draw(keys[4], (D, KVH * HD), D ** -0.5, 0.09375, ((1, 8),)),
        "o_weight": bell_draw(keys[5], (KVH * QPK * HD, D), HD ** -0.5, 0.5, ((0, 8),)),
        "prompt_keys": draw_prompt_keys(jax.random.fold_in(keys[9], 71), 0),
        "prompt_values": bell_draw(keys[7], (N_INST, PROMPT, KVH * HD), 1.0, 6.0, ((0, 32), (2, 8))),
        "owner_index": jax.random.randint(keys[8], (1,), 0, N_INST).astype(jnp.int32),
    }


epsilon = 1e-05

def rotate(tensor_in, positions):
    half_dim = tensor_in.shape[-1] // 2
    frequency = jnp.exp(-jnp.arange(half_dim).astype(jnp.float32) * (jnp.log(500000.0) / half_dim))
    angles = positions * frequency
    cosine = jnp.cos(angles)
    sine_part = jnp.sin(angles)
    first_half = tensor_in[..., :half_dim]
    second_half = tensor_in[..., half_dim:]
    return jnp.concatenate([first_half * cosine - second_half * sine_part, second_half * cosine + first_half * sine_part], axis=-1)

def project(new_states, attn_gain, q_weight, k_weight, v_weight, prompt_len):
    states = new_states.astype(jnp.float32)
    inv_norm = lax.rsqrt(lax.optimization_barrier(jnp.mean(states * states, axis=-1, keepdims=True)) + epsilon)
    normed = (states * inv_norm * attn_gain.astype(jnp.float32)).astype(jnp.bfloat16)
    step_count, samples, feature_dim = normed.shape
    flat_rows = normed.reshape(step_count * samples, feature_dim)
    queries = jnp.dot(flat_rows, q_weight, preferred_element_type=jnp.float32).reshape(step_count, samples, -1, HD)
    new_keys = jnp.dot(flat_rows, k_weight, preferred_element_type=jnp.float32).reshape(step_count, samples, -1, HD)
    new_values = jnp.dot(flat_rows, v_weight, preferred_element_type=jnp.float32).reshape(step_count, samples, -1, HD)
    positions = (prompt_len + jnp.arange(step_count)).astype(jnp.float32).reshape(step_count, 1, 1, 1)
    queries = rotate(queries, positions).astype(jnp.bfloat16)
    new_keys = rotate(new_keys, positions).astype(jnp.bfloat16)
    return (queries, new_keys, new_values.astype(jnp.bfloat16))

def prompt_part(query_rows, cache_keys, cache_values):
    head_dim = query_rows.shape[-1]
    scores = jnp.dot(query_rows, cache_keys.T, preferred_element_type=jnp.float32) * head_dim ** (-0.5)
    row_max = lax.optimization_barrier(jnp.max(scores, axis=1))
    raw_weights = jnp.exp(scores - row_max[:, None])
    row_sum = lax.optimization_barrier(jnp.sum(raw_weights, axis=1))
    weighted = jnp.dot(raw_weights.astype(jnp.bfloat16), cache_values, preferred_element_type=jnp.float32)
    return (row_max, row_sum, weighted)

def finish(queries, new_keys, new_values, row_max, row_sum, weighted):
    head_dim = queries.shape[-1]
    step_count = queries.shape[0]
    own_scores = jnp.einsum('tnqd,und->tnqu', queries.astype(jnp.float32), new_keys.astype(jnp.float32)) * head_dim ** (-0.5)
    step_ids = jnp.arange(step_count)
    causal = (step_ids[None, :] <= step_ids[:, None])[:, None, None, :]
    own_scores = jnp.where(causal, own_scores, -1e+30)
    joint_max = jnp.maximum(row_max, lax.optimization_barrier(jnp.max(own_scores, axis=-1)))
    raw_weights = jnp.where(causal, jnp.exp(own_scores - joint_max[..., None]), 0.0)
    rescale = jnp.exp(row_max - joint_max)
    denominator = row_sum * rescale + lax.optimization_barrier(jnp.sum(raw_weights, axis=-1))
    rounded = lax.optimization_barrier(raw_weights.astype(jnp.bfloat16)).astype(jnp.float32)
    numerator = weighted * rescale[..., None] + jnp.einsum('tnqu,und->tnqd', rounded, new_values.astype(jnp.float32))
    return (numerator / denominator[..., None]).astype(jnp.bfloat16)

def reference(new_states, attn_gain, q_weight, k_weight, v_weight, o_weight, prompt_keys, prompt_values, owner_index):
    prompt_len = prompt_keys.shape[1]
    queries, new_keys, new_values = project(new_states, attn_gain, q_weight, k_weight, v_weight, prompt_len)
    step_count, samples = (queries.shape[0], queries.shape[1])
    groups = new_keys.shape[2]
    queries = queries.reshape(step_count, samples, groups, -1, HD)
    heads_group = queries.shape[3]
    group_span = heads_group * HD
    chosen_keys = lax.dynamic_index_in_dim(prompt_keys, owner_index[0], 0, keepdims=False)
    chosen_values = lax.dynamic_index_in_dim(prompt_values, owner_index[0], 0, keepdims=False)
    feature_dim = o_weight.shape[1]
    result = jnp.zeros((step_count * samples, feature_dim), jnp.float32)
    query_shape = (step_count, samples, heads_group)
    for group_index in range(groups):
        group_queries = queries[:, :, group_index]
        row_max, row_sum, weighted = prompt_part(group_queries.reshape(-1, HD), chosen_keys[:, group_index * HD:(group_index + 1) * HD], chosen_values[:, group_index * HD:(group_index + 1) * HD])
        attended = finish(group_queries, new_keys[:, :, group_index], new_values[:, :, group_index], row_max.reshape(query_shape), row_sum.reshape(query_shape), weighted.reshape(query_shape + (HD,)))
        o_block = o_weight[group_index * group_span:(group_index + 1) * group_span]
        partial_value = jnp.dot(attended.reshape(step_count * samples, group_span), o_block, preferred_element_type=jnp.float32)
        result = result + lax.optimization_barrier(partial_value.astype(jnp.bfloat16)).astype(jnp.float32)
    return result.astype(jnp.bfloat16).reshape(step_count, samples, feature_dim)
```

```python
import jax
import jax.numpy as jnp
from jax import lax
from jax.sharding import PartitionSpec as P

HD = 128


epsilon = 1e-05


AXES = ("inst", "tp")
N_X, N_ZH, N_CORE = 4, 4, 2


def moves(tp_size, dx=0, dzh=0, dcore=0):
    pairs = []
    for x in range(N_X):
        for zh in range(N_ZH):
            for core in range(N_CORE):
                source = (x * N_ZH + zh) * N_CORE + core
                target = ((x + dx) % N_X * N_ZH + (zh + dzh) % N_ZH) * N_CORE + (core + dcore) % N_CORE
                pairs += [(source * tp_size + t, target * tp_size + t) for t in range(tp_size)]
    return pairs


def send(block, **delta):
    return lax.ppermute(block, AXES, moves(lax.axis_size("tp"), **delta))


def pick(pieces, index):
    chosen = pieces[0]
    for at in range(1, len(pieces)):
        chosen = jnp.where(index == at, pieces[at], chosen)
    return chosen


def spread(keys, values, root):
    me = lax.axis_index("inst")
    core, zh, x = me % N_CORE, me // N_CORE % N_ZH, me // (N_CORE * N_ZH)
    root_core, root_zh, root_x = root % N_CORE, root // N_CORE % N_ZH, root // (N_CORE * N_ZH)
    half = keys.shape[0] // 2
    quarter = half // N_X

    def part(start, size):
        return jnp.stack(
            [lax.dynamic_slice_in_dim(a, start, size, 0) for a in (keys, values)]
        )

    other = send(part((1 - core) * half, half), dcore=1)
    held = jnp.where(core == root_core, part(core * half, half), other)

    def slab(dx):
        return lax.dynamic_slice_in_dim(held, (x + dx) % N_X * quarter, quarter, 1)

    got = [slab(0)] + [send(slab(dx), dx=dx) for dx in range(1, N_X)]
    mine = pick(got, (x - root_x) % N_X)
    got = [mine] + [send(mine, dzh=dzh) for dzh in range(1, N_ZH)]
    mine = pick(got, (zh - root_zh) % N_ZH)
    row = jnp.concatenate([mine] + [send(mine, dx=dx) for dx in range(1, N_X)], axis=1)
    both = jnp.concatenate([row, send(row, dcore=1)], axis=1)
    return both[0], both[1]


def add_up(partial_value):
    ranks = lax.axis_size("tp")
    rows, features = partial_value.shape
    blocks = partial_value.reshape(rows, ranks, features // ranks).transpose(1, 0, 2)
    terms = lax.all_to_all(blocks, "tp", 0, 0)
    summed = jnp.sum(terms.astype(jnp.float32), axis=0).astype(jnp.bfloat16)
    copies = jnp.broadcast_to(summed, blocks.shape)
    gathered = lax.all_to_all(copies, "tp", 0, 0)
    return gathered.transpose(1, 0, 2).reshape(rows, features)


def rotate(tensor_in, positions):
    half_dim = tensor_in.shape[-1] // 2
    frequency = jnp.exp(-jnp.arange(half_dim).astype(jnp.float32) * (jnp.log(500000.0) / half_dim))
    angles = positions * frequency
    cosine = jnp.cos(angles)
    sine_part = jnp.sin(angles)
    first_half = tensor_in[..., :half_dim]
    second_half = tensor_in[..., half_dim:]
    return jnp.concatenate(
        [
            first_half * cosine - second_half * sine_part,
            second_half * cosine + first_half * sine_part,
        ],
        axis=-1,
    )


def project(new_states, attn_gain, q_weight, k_weight, v_weight, prompt_len):
    states = new_states.astype(jnp.float32)
    inv_norm = lax.rsqrt(jnp.mean(states * states, axis=-1, keepdims=True) + epsilon)
    normed = (states * inv_norm * attn_gain.astype(jnp.float32)).astype(jnp.bfloat16)
    step_count, samples, feature_dim = normed.shape
    flat_rows = normed.reshape(step_count * samples, feature_dim)
    queries = jnp.dot(flat_rows, q_weight, preferred_element_type=jnp.float32).reshape(
        step_count, samples, -1, HD
    )
    new_keys = jnp.dot(flat_rows, k_weight, preferred_element_type=jnp.float32).reshape(
        step_count, samples, HD
    )
    new_values = jnp.dot(flat_rows, v_weight, preferred_element_type=jnp.float32).reshape(
        step_count, samples, HD
    )
    positions = (prompt_len + jnp.arange(step_count)).astype(jnp.float32)
    queries = rotate(queries, positions.reshape(step_count, 1, 1, 1)).astype(jnp.bfloat16)
    new_keys = rotate(new_keys, positions.reshape(step_count, 1, 1)).astype(jnp.bfloat16)
    return (queries, new_keys, new_values.astype(jnp.bfloat16))


def prompt_part(query_rows, cache_keys, cache_values):
    head_dim = query_rows.shape[-1]
    scores = lax.dot_general(
        query_rows, cache_keys, (((1,), (1,)), ((), ())), preferred_element_type=jnp.float32
    ) * head_dim ** (-0.5)
    row_max = jnp.max(scores, axis=1)
    raw_weights = jnp.exp(scores - row_max[:, None])
    row_sum = jnp.sum(raw_weights, axis=1)
    weighted = jnp.dot(
        raw_weights.astype(jnp.bfloat16), cache_values, preferred_element_type=jnp.float32
    )
    return (row_max, row_sum, weighted)


def finish(queries, new_keys, new_values, row_max, row_sum, weighted):
    head_dim = queries.shape[-1]
    step_count = queries.shape[0]
    own_scores = jnp.einsum(
        "tnqd,und->tnqu", queries, new_keys, preferred_element_type=jnp.float32
    ) * head_dim ** (-0.5)
    step_ids = jnp.arange(step_count)
    causal = (step_ids[None, :] <= step_ids[:, None])[:, None, None, :]
    own_scores = jnp.where(causal, own_scores, -1e30)
    joint_max = jnp.maximum(row_max, jnp.max(own_scores, axis=-1))
    raw_weights = jnp.where(causal, jnp.exp(own_scores - joint_max[..., None]), 0.0)
    rescale = jnp.exp(row_max - joint_max)
    denominator = row_sum * rescale + jnp.sum(raw_weights, axis=-1)
    numerator = weighted * rescale[..., None] + jnp.einsum(
        "tnqu,und->tnqd",
        raw_weights.astype(jnp.bfloat16),
        new_values,
        preferred_element_type=jnp.float32,
    )
    return (numerator / denominator[..., None]).astype(jnp.bfloat16)


def on_device(
    new_states,
    attn_gain,
    q_weight,
    k_weight,
    v_weight,
    o_weight,
    prompt_keys,
    prompt_values,
    owner_index,
):
    prompt_len = prompt_keys.shape[1]
    queries, new_keys, new_values = project(
        new_states, attn_gain, q_weight, k_weight, v_weight, prompt_len
    )
    step_count, samples, head_count, head_dim = queries.shape
    local_keys = prompt_keys[0]
    local_values = prompt_values[0]
    root_index = owner_index[0]
    cache_keys, cache_values = spread(local_keys, local_values, root_index)
    step_parts = [
        prompt_part(queries[step_index].reshape(-1, head_dim), cache_keys, cache_values)
        for step_index in range(step_count)
    ]
    row_max = jnp.concatenate([piece[0] for piece in step_parts], axis=0)
    row_sum = jnp.concatenate([piece[1] for piece in step_parts], axis=0)
    weighted = jnp.concatenate([piece[2] for piece in step_parts], axis=0)
    query_shape = (step_count, samples, head_count)
    attended = finish(
        queries,
        new_keys,
        new_values,
        row_max.reshape(query_shape),
        row_sum.reshape(query_shape),
        weighted.reshape(query_shape + (head_dim,)),
    )
    partial_value = jnp.dot(
        attended.reshape(step_count * samples, head_count * head_dim),
        o_weight,
        preferred_element_type=jnp.float32,
    )
    summed = add_up(partial_value.astype(jnp.bfloat16))
    return summed.reshape(step_count, samples, o_weight.shape[1])


def solution(mesh):
    placed = (
        P(None, "inst", None),
        P(),
        P(None, "tp"),
        P(None, "tp"),
        P(None, "tp"),
        P("tp", None),
        P("inst", None, "tp"),
        P("inst", None, "tp"),
        P(),
    )
    return jax.shard_map(
        on_device, mesh=mesh, in_specs=placed, out_specs=P(None, "inst", None), check_vma=False
    )
```

```python
import jax
import jax.numpy as jnp
import numpy as np
from jax import lax
from jax.experimental import pallas as pl
from jax.experimental.pallas import tpu as pltpu
from jax.sharding import PartitionSpec as P

HD = 128


epsilon = 1e-05

AXES = ("inst", "tp")
N_X, N_ZH, N_CORE = 4, 4, 2
N_ZL, N_Y = 2, 4


def at(x, zh, core, zl, y):
    inst = (x % N_X * N_ZH + zh % N_ZH) * N_CORE + core % N_CORE
    return inst * (N_ZL * N_Y) + zl % N_ZL * N_Y + y % N_Y


def send(block, dx=0, dzh=0, dcore=0, dzl=0, dy=0, only=lambda x, zh, core: True):
    pairs = [
        (at(x, zh, core, zl, y), at(x + dx, zh + dzh, core + dcore, zl + dzl, y + dy))
        for x in range(N_X)
        for zh in range(N_ZH)
        for core in range(N_CORE)
        for zl in range(N_ZL)
        for y in range(N_Y)
        if only(x, zh, core)
    ]
    return lax.ppermute(block, AXES, pairs)


def scatter(pieces, x, core, root_x, root_core):
    def branch(from_x, from_core):
        def run(pieces):
            here = lambda x, zh, core: x == from_x and core == from_core
            mine = pieces[from_x * N_CORE + from_core]
            for dx in (2, 1, 3, 0):
                for dcore in (1, 0):
                    if dx or dcore:
                        to_x, to_core = (from_x + dx) % N_X, (from_core + dcore) % N_CORE
                        got = send(pieces[to_x * N_CORE + to_core], dx=dx, dcore=dcore, only=here)
                        mine = jnp.where((x == to_x) & (core == to_core), got, mine)
            return mine

        return run

    branches = [branch(a, b) for a in range(N_X) for b in range(N_CORE)]
    return lax.switch(root_x * N_CORE + root_core, branches, pieces)


def to_rows(piece, zh, root_zh):
    def branch(from_zh):
        def run(piece):
            here = lambda x, zh, core: zh == from_zh
            mine = piece
            for dzh in (2, 1, 3):
                got = send(piece, dzh=dzh, only=here)
                mine = jnp.where(zh == (from_zh + dzh) % N_ZH, got, mine)
            return mine

        return run

    return lax.switch(root_zh, [branch(a) for a in range(N_ZH)], piece)


def own_piece(keys, values, root):
    me = lax.axis_index("inst")
    core, zh, x = me % N_CORE, me // N_CORE % N_ZH, me // (N_CORE * N_ZH)
    root_core, root_zh, root_x = root % N_CORE, root // N_CORE % N_ZH, root // (N_CORE * N_ZH)
    parts = N_X * N_CORE
    pieces = jnp.stack(
        [a.reshape(parts, a.shape[0] // parts, a.shape[1]) for a in (keys, values)], axis=1
    )
    return to_rows(scatter(pieces, x, core, root_x, root_core), zh, root_zh)


def from_row(piece):
    row = jnp.stack([piece] + [send(piece, dx=dx) for dx in (2, 1, 3)])
    return row, send(row, dcore=1)


def project(new_states, attn_gain, q_weight, k_weight, v_weight, prompt_len):
    step_count, samples, feature_dim = new_states.shape
    rows = step_count * samples
    q_width, head_dim = q_weight.shape[1], k_weight.shape[1]
    heads, half = q_width // head_dim, head_dim // 2
    depth = 512
    frequency = np.exp(-np.arange(half) * (np.log(500000.0) / half))
    angles = (prompt_len + np.repeat(np.arange(step_count), samples))[:, None] * frequency
    cosine = np.concatenate([np.cos(angles)] * 2, axis=1).astype(np.float32)
    sine = np.concatenate([-np.sin(angles), np.sin(angles)], axis=1).astype(np.float32)

    def kernel(x_ref, gain_ref, cos_ref, sin_ref, wq_ref, wk_ref, wv_ref, q_ref, k_ref, v_ref, inv, acc):
        step = pl.program_id(0)

        @pl.when(step == 0)
        def _():
            states = x_ref[...].astype(jnp.float32)
            inv[...] = lax.rsqrt(jnp.mean(states * states, axis=-1, keepdims=True) + epsilon)
            acc[...] = jnp.zeros_like(acc)

        columns = pl.ds(pl.multiple_of(step * depth, depth), depth)
        states = x_ref[:, columns].astype(jnp.float32)
        gain = gain_ref[:, columns].astype(jnp.float32)
        normed = (states * inv[...] * gain).astype(jnp.bfloat16)
        at_column = 0
        for w_ref in (wq_ref, wk_ref, wv_ref):
            width = w_ref.shape[1]
            acc[:, at_column : at_column + width] += jnp.dot(
                normed, w_ref[...], preferred_element_type=jnp.float32
            )
            at_column += width

        @pl.when(step == pl.num_programs(0) - 1)
        def _():
            def rotated(block):
                swapped = pltpu.roll(block, half, 1)
                return (block * cos_ref[...] + swapped * sin_ref[...]).astype(jnp.bfloat16)

            for head in range(heads):
                q_ref[head] = rotated(acc[:, head * head_dim : (head + 1) * head_dim])
            k_ref[...] = rotated(acc[:, q_width : q_width + head_dim])
            v_ref[...] = acc[:, q_width + head_dim :].astype(jnp.bfloat16)

    whole = lambda *shape: pl.BlockSpec(shape, lambda i: (0,) * len(shape))
    weight = lambda width: pl.BlockSpec((depth, width), lambda i: (i, 0))
    return pl.pallas_call(
        kernel,
        grid=(feature_dim // depth,),
        in_specs=[
            whole(rows, feature_dim),
            whole(1, feature_dim),
            whole(rows, head_dim),
            whole(rows, head_dim),
            weight(q_width),
            weight(head_dim),
            weight(head_dim),
        ],
        out_specs=[whole(heads, rows, head_dim), whole(rows, head_dim), whole(rows, head_dim)],
        out_shape=[
            jax.ShapeDtypeStruct((heads, rows, head_dim), jnp.bfloat16),
            jax.ShapeDtypeStruct((rows, head_dim), jnp.bfloat16),
            jax.ShapeDtypeStruct((rows, head_dim), jnp.bfloat16),
        ],
        scratch_shapes=[
            pltpu.VMEM((rows, 1), jnp.float32),
            pltpu.VMEM((rows, q_width + 2 * head_dim), jnp.float32),
        ],
        compiler_params=pltpu.CompilerParams(vmem_limit_bytes=24 * 2**20),
        cost_estimate=pl.CostEstimate(
            flops=2 * rows * feature_dim * (q_width + 2 * head_dim),
            bytes_accessed=2 * feature_dim * (rows + q_width + 2 * head_dim),
            transcendentals=0,
        ),
    )(
        new_states.reshape(rows, feature_dim),
        attn_gain.reshape(1, feature_dim),
        cosine,
        sine,
        q_weight,
        k_weight,
        v_weight,
    )


def attend(queries, new_keys, new_values, row_kv, other_kv, o_weight, step_count):
    heads, rows, head_dim = queries.shape
    samples = rows // step_count
    features = o_weight.shape[1]
    width = features // N_Y
    scale = head_dim**-0.5
    pieces, _, positions, _ = row_kv.shape

    def kernel(y_ref, q_ref, k_ref, v_ref, row_ref, other_ref, o_hbm, *rest):
        out_refs, (o_vmem, scores, sems) = rest[:N_Y], rest[N_Y:]
        copies = []
        for d in range(N_Y):
            block = lax.rem(y_ref[0] + d, N_Y) * width
            copies.append(
                pltpu.make_async_copy(
                    o_hbm.at[:, pl.ds(pl.multiple_of(block, width), width)], o_vmem.at[d], sems.at[d]
                )
            )
            copies[-1].start()
        step_of = lax.broadcasted_iota(jnp.int32, (rows, 1), 0) // samples
        keys_of = [jnp.concatenate([k_ref[u * samples : (u + 1) * samples]] * step_count, axis=0).astype(jnp.float32) for u in range(step_count)]
        values_of = [jnp.concatenate([v_ref[u * samples : (u + 1) * samples]] * step_count, axis=0).astype(jnp.float32) for u in range(step_count)]
        attended = []
        for head in range(heads):
            q = q_ref[head]
            blocks = [(ref, p) for ref in (row_ref, other_ref) for p in range(pieces)]
            row_max = None
            for i, (ref, p) in enumerate(blocks):
                s = lax.dot_general(q, ref[p, 0], (((1,), (1,)), ((), ())), preferred_element_type=jnp.float32) * scale
                scores[head % 2, :, i * positions : (i + 1) * positions] = s
                top = jnp.max(s, axis=1, keepdims=True)
                row_max = top if row_max is None else jnp.maximum(row_max, top)
            row_sum = jnp.zeros((rows, 1), jnp.float32)
            weighted = jnp.zeros((rows, head_dim), jnp.float32)
            for i, (ref, p) in enumerate(blocks):
                e = jnp.exp(scores[head % 2, :, i * positions : (i + 1) * positions] - row_max)
                row_sum += jnp.sum(e, axis=1, keepdims=True)
                weighted += jnp.dot(e.astype(jnp.bfloat16), ref[p, 1], preferred_element_type=jnp.float32)
            q32 = q.astype(jnp.float32)
            joint_max, own = row_max, []
            for u in range(step_count):
                s = jnp.sum(q32 * keys_of[u], axis=1, keepdims=True) * scale
                s = jnp.where(step_of >= u, s, -1e30)
                joint_max = jnp.maximum(joint_max, s)
                own.append(s)
            rescale = jnp.exp(row_max - joint_max)
            denominator = row_sum * rescale
            numerator = weighted * rescale
            for u in range(step_count):
                e = jnp.where(step_of >= u, jnp.exp(own[u] - joint_max), 0.0)
                denominator += e
                numerator += e.astype(jnp.bfloat16).astype(jnp.float32) * values_of[u]
            attended.append((numerator / denominator).astype(jnp.bfloat16))
        attended = jnp.concatenate(attended, axis=1)
        for d in (2, 1, 3, 0):
            copies[d].wait()
            out_refs[d][...] = jnp.dot(attended, o_vmem[d], preferred_element_type=jnp.float32).astype(jnp.bfloat16)

    vmem = pl.BlockSpec(memory_space=pltpu.VMEM)
    return pl.pallas_call(
        kernel,
        in_specs=[pl.BlockSpec(memory_space=pltpu.SMEM)] + [vmem] * 5 + [pl.BlockSpec(memory_space=pl.ANY)],
        out_specs=[vmem] * N_Y,
        out_shape=[jax.ShapeDtypeStruct((rows, width), jnp.bfloat16)] * N_Y,
        scratch_shapes=[
            pltpu.VMEM((N_Y, o_weight.shape[0], width), jnp.bfloat16),
            pltpu.VMEM((2, rows, 2 * pieces * positions), jnp.float32),
            pltpu.SemaphoreType.DMA((N_Y,)),
        ],
        compiler_params=pltpu.CompilerParams(vmem_limit_bytes=24 * 2**20),
        cost_estimate=pl.CostEstimate(
            flops=2 * rows * features * o_weight.shape[0] + 8 * heads * rows * pieces * positions * head_dim,
            bytes_accessed=2 * o_weight.size + 4 * row_kv.size,
            transcendentals=0,
        ),
    )(lax.axis_index("tp").reshape(1) % N_Y, queries, new_keys, new_values, row_kv, other_kv, o_weight)


def add_up(blocks):
    got = [blocks[0]] + [send(blocks[d], dy=d) for d in (2, 1, 3)]
    along_y = sum(a.astype(jnp.float32) for a in got).astype(jnp.bfloat16)
    across = send(along_y, dzl=1)
    block = (along_y.astype(jnp.float32) + across.astype(jnp.float32)).astype(jnp.bfloat16)
    return [block] + [send(block, dy=d) for d in (1, 2, 3)]


def lay_out(blocks):
    rows, width = blocks[0].shape

    def kernel(y_ref, *rest):
        ins, out, sems = rest[:N_Y], rest[N_Y], rest[N_Y + 1]
        copies = []
        for d in range(N_Y):
            column = lax.rem(y_ref[0] + N_Y - d, N_Y) * width
            copies.append(
                pltpu.make_async_copy(
                    ins[d], out.at[:, pl.ds(pl.multiple_of(column, width), width)], sems.at[d]
                )
            )
            copies[-1].start()
        for copy in copies:
            copy.wait()

    anywhere = pl.BlockSpec(memory_space=pl.ANY)
    return pl.pallas_call(
        kernel,
        in_specs=[pl.BlockSpec(memory_space=pltpu.SMEM)] + [anywhere] * N_Y,
        out_specs=anywhere,
        out_shape=jax.ShapeDtypeStruct((rows, N_Y * width), blocks[0].dtype),
        scratch_shapes=[pltpu.SemaphoreType.DMA((N_Y,))],
    )(lax.axis_index("tp").reshape(1) % N_Y, *blocks)


def on_device(
    new_states,
    attn_gain,
    q_weight,
    k_weight,
    v_weight,
    o_weight,
    prompt_keys,
    prompt_values,
    owner_index,
):
    step_count, samples, _ = new_states.shape
    piece = own_piece(prompt_keys[0], prompt_values[0], owner_index[0])
    new_states, piece = lax.optimization_barrier((new_states, piece))
    row_kv, other_kv = from_row(piece)
    queries, new_keys, new_values = project(
        new_states, attn_gain, q_weight, k_weight, v_weight, prompt_keys.shape[1]
    )
    partial_blocks = attend(queries, new_keys, new_values, row_kv, other_kv, o_weight, step_count)
    summed = lay_out(add_up(partial_blocks))
    return summed.reshape(step_count, samples, o_weight.shape[1])


def solution(mesh):
    placed = (
        P(None, "inst", None),
        P(),
        P(None, "tp"),
        P(None, "tp"),
        P(None, "tp"),
        P("tp", None),
        P("inst", None, "tp"),
        P("inst", None, "tp"),
        P(),
    )
    return jax.shard_map(
        on_device, mesh=mesh, in_specs=placed, out_specs=P(None, "inst", None), check_vma=False
    )
```

```python
import jax
import jax.numpy as jnp
import numpy as np
from jax import lax
from jax.experimental import pallas as pl
from jax.experimental.pallas import tpu as pltpu
from jax.sharding import PartitionSpec as P

HD = 128


epsilon = 1e-05

AXES = ("inst", "tp")
N_X, N_ZH, N_CORE = 4, 4, 2
N_ZL, N_Y = 2, 4


def at(x, zh, core, zl, y):
    inst = (x % N_X * N_ZH + zh % N_ZH) * N_CORE + core % N_CORE
    return inst * (N_ZL * N_Y) + zl % N_ZL * N_Y + y % N_Y


def send(block, dx=0, dzh=0, dcore=0, dzl=0, dy=0, only=lambda x, zh, core: True):
    pairs = [
        (at(x, zh, core, zl, y), at(x + dx, zh + dzh, core + dcore, zl + dzl, y + dy))
        for x in range(N_X)
        for zh in range(N_ZH)
        for core in range(N_CORE)
        for zl in range(N_ZL)
        for y in range(N_Y)
        if only(x, zh, core)
    ]
    return lax.ppermute(block, AXES, pairs)


def from_owner(pieces, at_place, root_place, size, only):
    def branch(place):
        def run(pieces):
            mine = pieces[0]
            for d in (2, 1, 3):
                got = only(pieces[d], d, place)
                mine = jnp.where(at_place == (place + d) % size, got, mine)
            return mine

        return run

    return lax.switch(root_place, [branch(a) for a in range(size)], pieces)


def broadcast(keys, values, root):
    me = lax.axis_index("inst")
    core, zh, x = me % N_CORE, me // N_CORE % N_ZH, me // (N_CORE * N_ZH)
    root_core, root_zh, root_x = root % N_CORE, root // N_CORE % N_ZH, root // (N_CORE * N_ZH)
    has_keys = core == root_core
    held = jnp.where(has_keys, keys, send(values, dcore=1))
    quarter = keys.shape[0] // N_X
    slabs = [held[d * quarter : (d + 1) * quarter] for d in range(N_X)]
    along_x = lambda a, d, place: send(a, dx=d, only=lambda x, zh, core: x == place)
    along_z = lambda a, d, place: send(a, dzh=d, only=lambda x, zh, core: zh == place)
    mine = from_owner(slabs, x, root_x, N_X, along_x)
    mine = from_owner([mine] * N_ZH, zh, root_zh, N_ZH, along_z)
    return mine, has_keys


def from_row(mine):
    row = [mine] + [send(mine, dx=dx) for dx in (1, 3, 2)]
    return row, [send(a, dcore=1) for a in row]


def project(new_states, attn_gain, q_weight, k_weight, v_weight, prompt_len):
    step_count, samples, feature_dim = new_states.shape
    rows = step_count * samples
    q_width, head_dim = q_weight.shape[1], k_weight.shape[1]
    heads, half = q_width // head_dim, head_dim // 2
    depth = 512
    frequency = np.exp(-np.arange(half) * (np.log(500000.0) / half))
    angles = (prompt_len + np.repeat(np.arange(step_count), samples))[:, None] * frequency
    cosine = np.concatenate([np.cos(angles)] * 2, axis=1).astype(np.float32)
    sine = np.concatenate([-np.sin(angles), np.sin(angles)], axis=1).astype(np.float32)

    def kernel(x_ref, gain_ref, cos_ref, sin_ref, wq_ref, wk_ref, wv_ref, q_ref, k_ref, v_ref, inv, acc):
        step = pl.program_id(0)

        @pl.when(step == 0)
        def _():
            states = x_ref[...].astype(jnp.float32)
            inv[...] = lax.rsqrt(jnp.mean(states * states, axis=-1, keepdims=True) + epsilon)
            acc[...] = jnp.zeros_like(acc)

        columns = pl.ds(pl.multiple_of(step * depth, depth), depth)
        states = x_ref[:, columns].astype(jnp.float32)
        gain = gain_ref[:, columns].astype(jnp.float32)
        normed = (states * inv[...] * gain).astype(jnp.bfloat16)
        at_column = 0
        for w_ref in (wq_ref, wk_ref, wv_ref):
            width = w_ref.shape[1]
            acc[:, at_column : at_column + width] += jnp.dot(
                normed, w_ref[...], preferred_element_type=jnp.float32
            )
            at_column += width

        @pl.when(step == pl.num_programs(0) - 1)
        def _():
            def rotated(block):
                swapped = pltpu.roll(block, half, 1)
                return (block * cos_ref[...] + swapped * sin_ref[...]).astype(jnp.bfloat16)

            for head in range(heads):
                q_ref[head] = rotated(acc[:, head * head_dim : (head + 1) * head_dim])
            k_ref[...] = rotated(acc[:, q_width : q_width + head_dim])
            v_ref[...] = acc[:, q_width + head_dim :].astype(jnp.bfloat16)

    whole = lambda *shape: pl.BlockSpec(shape, lambda i: (0,) * len(shape))
    weight = lambda width: pl.BlockSpec((depth, width), lambda i: (i, 0))
    return pl.pallas_call(
        kernel,
        grid=(feature_dim // depth,),
        in_specs=[
            whole(rows, feature_dim),
            whole(1, feature_dim),
            whole(rows, head_dim),
            whole(rows, head_dim),
            weight(q_width),
            weight(head_dim),
            weight(head_dim),
        ],
        out_specs=[whole(heads, rows, head_dim), whole(rows, head_dim), whole(rows, head_dim)],
        out_shape=[
            jax.ShapeDtypeStruct((heads, rows, head_dim), jnp.bfloat16),
            jax.ShapeDtypeStruct((rows, head_dim), jnp.bfloat16),
            jax.ShapeDtypeStruct((rows, head_dim), jnp.bfloat16),
        ],
        scratch_shapes=[
            pltpu.VMEM((rows, 1), jnp.float32),
            pltpu.VMEM((rows, q_width + 2 * head_dim), jnp.float32),
        ],
        compiler_params=pltpu.CompilerParams(vmem_limit_bytes=24 * 2**20),
        cost_estimate=pl.CostEstimate(
            flops=2 * rows * feature_dim * (q_width + 2 * head_dim),
            bytes_accessed=2 * feature_dim * (rows + q_width + 2 * head_dim),
            transcendentals=0,
        ),
    )(
        new_states.reshape(rows, feature_dim),
        attn_gain.reshape(1, feature_dim),
        cosine,
        sine,
        q_weight,
        k_weight,
        v_weight,
    )


def attend(queries, new_keys, new_values, row, other, has_keys, o_weight, step_count):
    heads, rows, head_dim = queries.shape
    samples = rows // step_count
    features = o_weight.shape[1]
    width = features // N_Y
    scale = head_dim**-0.5
    pieces, positions = len(row), row[0].shape[0]

    def kernel(place_ref, q_ref, k_ref, v_ref, o_ref, *rest):
        row_refs, other_refs, rest = rest[:pieces], rest[pieces : 2 * pieces], rest[2 * pieces :]
        out_refs, (keys, values, scores) = rest[:N_Y], rest[N_Y:]

        @pl.when(place_ref[1] == 1)
        def _():
            for p in range(pieces):
                keys[p], values[p] = row_refs[p][...], other_refs[p][...]

        @pl.when(place_ref[1] == 0)
        def _():
            for p in range(pieces):
                keys[p], values[p] = other_refs[p][...], row_refs[p][...]

        step_of = lax.broadcasted_iota(jnp.int32, (rows, 1), 0) // samples
        keys_of = [jnp.concatenate([k_ref[u * samples : (u + 1) * samples]] * step_count, axis=0).astype(jnp.float32) for u in range(step_count)]
        values_of = [jnp.concatenate([v_ref[u * samples : (u + 1) * samples]] * step_count, axis=0).astype(jnp.float32) for u in range(step_count)]
        q_all = q_ref[...].reshape(heads * rows, head_dim)
        row_max = None
        for i in range(pieces):
            s = lax.dot_general(q_all, keys[i], (((1,), (1,)), ((), ())), preferred_element_type=jnp.float32) * scale
            scores[i] = s
            top = jnp.max(s, axis=1, keepdims=True)
            row_max = top if row_max is None else jnp.maximum(row_max, top)
        row_sum = jnp.zeros((heads * rows, 1), jnp.float32)
        weighted = jnp.zeros((heads * rows, head_dim), jnp.float32)
        for i in range(pieces):
            e = jnp.exp(scores[i] - row_max)
            row_sum += jnp.sum(e, axis=1, keepdims=True)
            weighted += jnp.dot(e.astype(jnp.bfloat16), values[i], preferred_element_type=jnp.float32)
        attended = []
        for head in range(heads):
            part = slice(head * rows, (head + 1) * rows)
            q32 = q_ref[head].astype(jnp.float32)
            joint_max, own = row_max[part], []
            for u in range(step_count):
                s = jnp.sum(q32 * keys_of[u], axis=1, keepdims=True) * scale
                s = jnp.where(step_of >= u, s, -1e30)
                joint_max = jnp.maximum(joint_max, s)
                own.append(s)
            rescale = jnp.exp(row_max[part] - joint_max)
            denominator = row_sum[part] * rescale
            numerator = weighted[part] * rescale
            for u in range(step_count):
                e = jnp.where(step_of >= u, jnp.exp(own[u] - joint_max), 0.0)
                denominator += e
                numerator += e.astype(jnp.bfloat16).astype(jnp.float32) * values_of[u]
            attended.append((numerator / denominator).astype(jnp.bfloat16))
        attended = jnp.concatenate(attended, axis=1)
        for d in (2, 1, 3, 0):
            column = lax.rem(place_ref[0] + d, N_Y) * width
            o_block = o_ref[:, pl.ds(pl.multiple_of(column, width), width)]
            out_refs[d][...] = jnp.dot(attended, o_block, preferred_element_type=jnp.float32).astype(jnp.bfloat16)

    place = jnp.stack([lax.axis_index("tp") % N_Y, has_keys.astype(jnp.int32)])
    vmem = pl.BlockSpec(memory_space=pltpu.VMEM)
    return pl.pallas_call(
        kernel,
        in_specs=[pl.BlockSpec(memory_space=pltpu.SMEM)] + [vmem] * (4 + 2 * pieces),
        out_specs=[vmem] * N_Y,
        out_shape=[jax.ShapeDtypeStruct((rows, width), jnp.bfloat16)] * N_Y,
        scratch_shapes=[
            pltpu.VMEM((pieces, positions, head_dim), jnp.bfloat16),
            pltpu.VMEM((pieces, positions, head_dim), jnp.bfloat16),
            pltpu.VMEM((pieces, heads * rows, positions), jnp.float32),
        ],
        compiler_params=pltpu.CompilerParams(vmem_limit_bytes=24 * 2**20),
        cost_estimate=pl.CostEstimate(
            flops=2 * rows * features * o_weight.shape[0] + 8 * heads * rows * pieces * positions * head_dim,
            bytes_accessed=2 * o_weight.size + 4 * pieces * row[0].size,
            transcendentals=0,
        ),
    )(place, queries, new_keys, new_values, o_weight, *row, *other)


def add_up(blocks):
    got = [blocks[0]] + [send(blocks[d], dy=d) for d in (2, 1, 3)]
    along_y = sum(a.astype(jnp.float32) for a in got).astype(jnp.bfloat16)
    across = send(along_y, dzl=1)
    block = (along_y.astype(jnp.float32) + across.astype(jnp.float32)).astype(jnp.bfloat16)
    return [block] + [send(block, dy=d) for d in (1, 2, 3)]


def lay_out(blocks):
    rows, width = blocks[0].shape

    def kernel(y_ref, *rest):
        ins, out = rest[:N_Y], rest[N_Y]
        for d in range(N_Y):
            column = lax.rem(y_ref[0] + N_Y - d, N_Y) * width
            out[:, pl.ds(pl.multiple_of(column, width), width)] = ins[d][...]

    vmem = pl.BlockSpec(memory_space=pltpu.VMEM)
    return pl.pallas_call(
        kernel,
        in_specs=[pl.BlockSpec(memory_space=pltpu.SMEM)] + [vmem] * N_Y,
        out_specs=vmem,
        out_shape=jax.ShapeDtypeStruct((rows, N_Y * width), blocks[0].dtype),
        compiler_params=pltpu.CompilerParams(vmem_limit_bytes=8 * 2**20),
    )(lax.axis_index("tp").reshape(1) % N_Y, *blocks)


def on_device(
    new_states,
    attn_gain,
    q_weight,
    k_weight,
    v_weight,
    o_weight,
    prompt_keys,
    prompt_values,
    owner_index,
):
    step_count, samples, _ = new_states.shape
    piece, has_keys = broadcast(prompt_keys[0], prompt_values[0], owner_index[0])
    new_states, piece = lax.optimization_barrier((new_states, piece))
    row, other = from_row(piece)
    queries, new_keys, new_values = project(
        new_states, attn_gain, q_weight, k_weight, v_weight, prompt_keys.shape[1]
    )
    partial_blocks = attend(queries, new_keys, new_values, row, other, has_keys, o_weight, step_count)
    summed = lay_out(add_up(partial_blocks))
    return summed.reshape(step_count, samples, o_weight.shape[1])


def solution(mesh):
    placed = (
        P(None, "inst", None),
        P(),
        P(None, "tp"),
        P(None, "tp"),
        P(None, "tp"),
        P("tp", None),
        P("inst", None, "tp"),
        P("inst", None, "tp"),
        P(),
    )
    return jax.shard_map(
        on_device, mesh=mesh, in_specs=placed, out_specs=P(None, "inst", None), check_vma=False
    )
```

```python
import jax
import jax.numpy as jnp
import numpy as np
from jax import lax
from jax.experimental import pallas as pl
from jax.experimental.pallas import tpu as pltpu
from jax.sharding import PartitionSpec as P

HD = 128
PARTS = 2


epsilon = 1e-05

AXES = ("inst", "tp")
N_X, N_ZH, N_CORE = 4, 4, 2
N_ZL, N_Y = 2, 4


def at(x, zh, core, zl, y):
    inst = (x % N_X * N_ZH + zh % N_ZH) * N_CORE + core % N_CORE
    return inst * (N_ZL * N_Y) + zl % N_ZL * N_Y + y % N_Y


def send(block, dx=0, dzh=0, dcore=0, dzl=0, dy=0, only=lambda x, zh, core: True):
    pairs = [
        (at(x, zh, core, zl, y), at(x + dx, zh + dzh, core + dcore, zl + dzl, y + dy))
        for x in range(N_X)
        for zh in range(N_ZH)
        for core in range(N_CORE)
        for zl in range(N_ZL)
        for y in range(N_Y)
        if only(x, zh, core)
    ]
    return lax.ppermute(block, AXES, pairs)


def over_rows(piece, zh, root_zh):
    def branch(from_zh):
        def run(piece):
            mine = piece
            for d in (2, 1, 3):
                got = send(piece, dzh=d, only=lambda x, zh, core: zh == from_zh)
                mine = jnp.where(zh == (from_zh + d) % N_ZH, got, mine)
            return mine

        return run

    return lax.switch(root_zh, [branch(a) for a in range(N_ZH)], piece)


def broadcast(keys, values, root):
    me = lax.axis_index("inst")
    core, zh, x = me % N_CORE, me // N_CORE % N_ZH, me // (N_CORE * N_ZH)
    root_core, root_zh, root_x = root % N_CORE, root // N_CORE % N_ZH, root // (N_CORE * N_ZH)
    has_keys = core == root_core
    got_values = send(values, dcore=1)
    quarter = keys.shape[0] // N_X

    def slab(d):
        part = slice(d * quarter, (d + 1) * quarter)
        return jnp.where(has_keys, keys[part], got_values[part])

    got = {d: send(slab(d), dx=d) for d in (2, 1, 3)}
    mine = slab(0)
    for d in (2, 1, 3):
        mine = jnp.where((x - root_x) % N_X == d, got[d], mine)
    mine = over_rows(mine, zh, root_zh)
    return mine, has_keys


def from_row(mine):
    row = [mine] + [send(mine, dx=dx) for dx in (1, 3, 2)]
    return row, [send(a, dcore=1) for a in row]


def project(new_states, attn_gain, q_weight, k_weight, v_weight, prompt_len):
    step_count, samples, feature_dim = new_states.shape
    rows = step_count * samples
    q_width, head_dim = q_weight.shape[1], k_weight.shape[1]
    heads, half = q_width // head_dim, head_dim // 2
    depth = 512
    frequency = np.exp(-np.arange(half) * (np.log(500000.0) / half))
    angles = (prompt_len + np.repeat(np.arange(step_count), samples))[:, None] * frequency
    cosine = np.concatenate([np.cos(angles)] * 2, axis=1).astype(np.float32)
    sine = np.concatenate([-np.sin(angles), np.sin(angles)], axis=1).astype(np.float32)

    def kernel(x_ref, gain_ref, cos_ref, sin_ref, wq_ref, wk_ref, wv_ref, q_ref, k_ref, v_ref, inv, acc):
        step = pl.program_id(0)

        @pl.when(step == 0)
        def _():
            states = x_ref[...].astype(jnp.float32)
            inv[...] = lax.rsqrt(jnp.mean(states * states, axis=-1, keepdims=True) + epsilon)
            acc[...] = jnp.zeros_like(acc)

        columns = pl.ds(pl.multiple_of(step * depth, depth), depth)
        states = x_ref[:, columns].astype(jnp.float32)
        gain = gain_ref[:, columns].astype(jnp.float32)
        normed = (states * inv[...] * gain).astype(jnp.bfloat16)
        at_column = 0
        for w_ref in (wq_ref, wk_ref, wv_ref):
            width = w_ref.shape[1]
            acc[:, at_column : at_column + width] += jnp.dot(
                normed, w_ref[...], preferred_element_type=jnp.float32
            )
            at_column += width

        @pl.when(step == pl.num_programs(0) - 1)
        def _():
            def rotated(block):
                swapped = pltpu.roll(block, half, 1)
                return (block * cos_ref[...] + swapped * sin_ref[...]).astype(jnp.bfloat16)

            for head in range(heads):
                q_ref[head] = rotated(acc[:, head * head_dim : (head + 1) * head_dim])
            k_ref[...] = rotated(acc[:, q_width : q_width + head_dim])
            v_ref[...] = acc[:, q_width + head_dim :].astype(jnp.bfloat16)

    whole = lambda *shape: pl.BlockSpec(shape, lambda i: (0,) * len(shape))
    weight = lambda width: pl.BlockSpec((depth, width), lambda i: (i, 0))
    return pl.pallas_call(
        kernel,
        grid=(feature_dim // depth,),
        in_specs=[
            whole(rows, feature_dim),
            whole(1, feature_dim),
            whole(rows, head_dim),
            whole(rows, head_dim),
            weight(q_width),
            weight(head_dim),
            weight(head_dim),
        ],
        out_specs=[whole(heads, rows, head_dim), whole(rows, head_dim), whole(rows, head_dim)],
        out_shape=[
            jax.ShapeDtypeStruct((heads, rows, head_dim), jnp.bfloat16),
            jax.ShapeDtypeStruct((rows, head_dim), jnp.bfloat16),
            jax.ShapeDtypeStruct((rows, head_dim), jnp.bfloat16),
        ],
        scratch_shapes=[
            pltpu.VMEM((rows, 1), jnp.float32),
            pltpu.VMEM((rows, q_width + 2 * head_dim), jnp.float32),
        ],
        compiler_params=pltpu.CompilerParams(vmem_limit_bytes=24 * 2**20),
        cost_estimate=pl.CostEstimate(
            flops=2 * rows * feature_dim * (q_width + 2 * head_dim),
            bytes_accessed=2 * feature_dim * (rows + q_width + 2 * head_dim),
            transcendentals=0,
        ),
    )(
        new_states.reshape(rows, feature_dim),
        attn_gain.reshape(1, feature_dim),
        cosine,
        sine,
        q_weight,
        k_weight,
        v_weight,
    )


def attend(queries, new_keys, new_values, row, other, has_keys, o_weight, step_count):
    heads, rows, head_dim = queries.shape
    samples = rows // step_count
    features = o_weight.shape[1]
    width = features // (N_Y * PARTS)
    scale = head_dim**-0.5
    pieces, positions = len(row), row[0].shape[0]

    def kernel(place_ref, q_ref, k_ref, v_ref, o_ref, *rest):
        row_refs, other_refs, rest = rest[:pieces], rest[pieces : 2 * pieces], rest[2 * pieces :]
        out_refs, (keys, values, scores) = rest[: PARTS * N_Y], rest[PARTS * N_Y :]

        @pl.when(place_ref[1] == 1)
        def _():
            for p in range(pieces):
                keys[p], values[p] = row_refs[p][...], other_refs[p][...]

        @pl.when(place_ref[1] == 0)
        def _():
            for p in range(pieces):
                keys[p], values[p] = other_refs[p][...], row_refs[p][...]

        step_of = lax.broadcasted_iota(jnp.int32, (rows, 1), 0) // samples
        keys_of = [jnp.concatenate([k_ref[u * samples : (u + 1) * samples]] * step_count, axis=0).astype(jnp.float32) for u in range(step_count)]
        values_of = [jnp.concatenate([v_ref[u * samples : (u + 1) * samples]] * step_count, axis=0).astype(jnp.float32) for u in range(step_count)]
        q_all = q_ref[...].reshape(heads * rows, head_dim)
        row_max = None
        for i in range(pieces):
            s = lax.dot_general(q_all, keys[i], (((1,), (1,)), ((), ())), preferred_element_type=jnp.float32) * scale
            scores[i] = s
            top = jnp.max(s, axis=1, keepdims=True)
            row_max = top if row_max is None else jnp.maximum(row_max, top)
        row_sum = jnp.zeros((heads * rows, 1), jnp.float32)
        weighted = jnp.zeros((heads * rows, head_dim), jnp.float32)
        for i in range(pieces):
            e = jnp.exp(scores[i] - row_max)
            row_sum += jnp.sum(e, axis=1, keepdims=True)
            weighted += jnp.dot(e.astype(jnp.bfloat16), values[i], preferred_element_type=jnp.float32)
        attended = []
        for head in range(heads):
            part = slice(head * rows, (head + 1) * rows)
            q32 = q_ref[head].astype(jnp.float32)
            joint_max, own = row_max[part], []
            for u in range(step_count):
                s = jnp.sum(q32 * keys_of[u], axis=1, keepdims=True) * scale
                s = jnp.where(step_of >= u, s, -1e30)
                joint_max = jnp.maximum(joint_max, s)
                own.append(s)
            rescale = jnp.exp(row_max[part] - joint_max)
            denominator = row_sum[part] * rescale
            numerator = weighted[part] * rescale
            for u in range(step_count):
                e = jnp.where(step_of >= u, jnp.exp(own[u] - joint_max), 0.0)
                denominator += e
                numerator += e.astype(jnp.bfloat16).astype(jnp.float32) * values_of[u]
            attended.append((numerator / denominator).astype(jnp.bfloat16))
        attended = jnp.concatenate(attended, axis=1)
        for i in range(PARTS * N_Y):
            column = lax.rem(place_ref[0] + i % N_Y, N_Y) * (PARTS * width) + i // N_Y * width
            o_block = o_ref[:, pl.ds(pl.multiple_of(column, width), width)]
            out_refs[i][...] = jnp.dot(attended, o_block, preferred_element_type=jnp.float32).astype(jnp.bfloat16)

    place = jnp.stack([lax.axis_index("tp") % N_Y, has_keys.astype(jnp.int32)])
    vmem = pl.BlockSpec(memory_space=pltpu.VMEM)
    return pl.pallas_call(
        kernel,
        in_specs=[pl.BlockSpec(memory_space=pltpu.SMEM)] + [vmem] * (4 + 2 * pieces),
        out_specs=[vmem] * (PARTS * N_Y),
        out_shape=[jax.ShapeDtypeStruct((rows, width), jnp.bfloat16)] * (PARTS * N_Y),
        scratch_shapes=[
            pltpu.VMEM((pieces, positions, head_dim), jnp.bfloat16),
            pltpu.VMEM((pieces, positions, head_dim), jnp.bfloat16),
            pltpu.VMEM((pieces, heads * rows, positions), jnp.float32),
        ],
        compiler_params=pltpu.CompilerParams(vmem_limit_bytes=24 * 2**20),
        cost_estimate=pl.CostEstimate(
            flops=2 * rows * features * o_weight.shape[0] + 8 * heads * rows * pieces * positions * head_dim,
            bytes_accessed=2 * o_weight.size + 4 * pieces * row[0].size,
            transcendentals=0,
        ),
    )(place, queries, new_keys, new_values, o_weight, *row, *other)


def add_up(parts):
    got = [[blocks[0]] + [send(blocks[d], dy=d) for d in (1, 2, 3)] for blocks in parts]
    along_y = [sum(a.astype(jnp.float32) for a in terms).astype(jnp.bfloat16) for terms in got]
    across = [send(a, dzl=1) for a in along_y]
    blocks = [
        (a.astype(jnp.float32) + b.astype(jnp.float32)).astype(jnp.bfloat16)
        for a, b in zip(along_y, across)
    ]
    return [[block] + [send(block, dy=d) for d in (1, 2, 3)] for block in blocks]


def lay_out(parts):
    rows, width = parts[0][0].shape

    def kernel(y_ref, *rest):
        ins, out = rest[: PARTS * N_Y], rest[PARTS * N_Y]
        for i in range(PARTS * N_Y):
            column = lax.rem(y_ref[0] + N_Y - i % N_Y, N_Y) * (PARTS * width) + i // N_Y * width
            out[:, pl.ds(pl.multiple_of(column, width), width)] = ins[i][...]

    vmem = pl.BlockSpec(memory_space=pltpu.VMEM)
    return pl.pallas_call(
        kernel,
        in_specs=[pl.BlockSpec(memory_space=pltpu.SMEM)] + [vmem] * (PARTS * N_Y),
        out_specs=vmem,
        out_shape=jax.ShapeDtypeStruct((rows, PARTS * N_Y * width), parts[0][0].dtype),
        compiler_params=pltpu.CompilerParams(vmem_limit_bytes=8 * 2**20),
    )(lax.axis_index("tp").reshape(1) % N_Y, *[block for blocks in parts for block in blocks])


def on_device(
    new_states,
    attn_gain,
    q_weight,
    k_weight,
    v_weight,
    o_weight,
    prompt_keys,
    prompt_values,
    owner_index,
):
    step_count, samples, _ = new_states.shape
    piece, has_keys = broadcast(prompt_keys[0], prompt_values[0], owner_index[0])
    new_states, piece = lax.optimization_barrier((new_states, piece))
    row, other = from_row(piece)
    queries, new_keys, new_values = project(
        new_states, attn_gain, q_weight, k_weight, v_weight, prompt_keys.shape[1]
    )
    partial_blocks = attend(queries, new_keys, new_values, row, other, has_keys, o_weight, step_count)
    summed = lay_out(add_up([partial_blocks[i * N_Y : (i + 1) * N_Y] for i in range(PARTS)]))
    return summed.reshape(step_count, samples, o_weight.shape[1])


def solution(mesh):
    placed = (
        P(None, "inst", None),
        P(),
        P(None, "tp"),
        P(None, "tp"),
        P(None, "tp"),
        P("tp", None),
        P("inst", None, "tp"),
        P("inst", None, "tp"),
        P(),
    )
    return jax.shard_map(
        on_device, mesh=mesh, in_specs=placed, out_specs=P(None, "inst", None), check_vma=False
    )
```

```python
import jax
import jax.numpy as jnp
import numpy as np
from jax import lax
from jax.experimental import pallas as pl
from jax.experimental.pallas import tpu as pltpu
from jax.sharding import PartitionSpec as P

HD = 128
PARTS = 2
BRING_GRANT = 16
QKV_GRANT = 56
ROW_ORDER = (2, 3, 1)


epsilon = 1e-05

AXES = ("inst", "tp")
N_X, N_ZH, N_CORE = 4, 4, 2
N_ZL, N_Y = 2, 4


def at(x, zh, core, zl, y):
    inst = (x % N_X * N_ZH + zh % N_ZH) * N_CORE + core % N_CORE
    return inst * (N_ZL * N_Y) + zl % N_ZL * N_Y + y % N_Y


def send(block, dx=0, dzh=0, dcore=0, dzl=0, dy=0, only=lambda x, zh, core: True):
    pairs = [
        (at(x, zh, core, zl, y), at(x + dx, zh + dzh, core + dcore, zl + dzl, y + dy))
        for x in range(N_X)
        for zh in range(N_ZH)
        for core in range(N_CORE)
        for zl in range(N_ZL)
        for y in range(N_Y)
        if only(x, zh, core)
    ]
    return lax.ppermute(block, AXES, pairs)


VMEM = pl.BlockSpec(memory_space=pltpu.VMEM)
SMEM = pl.BlockSpec(memory_space=pltpu.SMEM)


def pick(pieces, index):
    def kernel(index_ref, *refs):
        for d, ref in enumerate(refs[:-1]):

            @pl.when(index_ref[0] == d)
            def _():
                refs[-1][...] = ref[...]

    return pl.pallas_call(
        kernel,
        in_specs=[SMEM] + [VMEM] * len(pieces),
        out_specs=VMEM,
        out_shape=jax.ShapeDtypeStruct(pieces[0].shape, pieces[0].dtype),
        compiler_params=pltpu.CompilerParams(vmem_limit_bytes=4 * 2**20),
    )(index.reshape(1), *pieces)


def slabs_of(first, keys, values):
    size, width = keys.shape[0] // N_X, keys.shape[1]

    def kernel(first_ref, keys_ref, values_ref, *slabs):
        for want, ref in ((1, keys_ref), (0, values_ref)):

            @pl.when(first_ref[0] == want)
            def _():
                for d in range(N_X):
                    slabs[d][...] = ref[d * size : (d + 1) * size]

    return pl.pallas_call(
        kernel,
        in_specs=[SMEM, VMEM, VMEM],
        out_specs=[VMEM] * N_X,
        out_shape=[jax.ShapeDtypeStruct((size, width), keys.dtype)] * N_X,
        compiler_params=pltpu.CompilerParams(vmem_limit_bytes=4 * 2**20),
    )(first.astype(jnp.int32).reshape(1), keys, values)


def over_rows(piece, zh, root_zh):
    def branch(from_zh):
        def run(piece):
            only = lambda x, zh, core: zh == from_zh
            got = {d: send(piece, dzh=d, only=only) for d in ROW_ORDER}
            place = sum(((from_zh + d) % N_ZH == zh) * (i + 1) for i, d in enumerate(ROW_ORDER))
            return pick([piece] + [got[d] for d in ROW_ORDER], place)

        return run

    return lax.switch(root_zh, [branch(a) for a in range(N_ZH)], piece)


def broadcast(keys, values, root, gain, beside):
    me = lax.axis_index("inst")
    core, zh, x = me % N_CORE, me // N_CORE % N_ZH, me // (N_CORE * N_ZH)
    root_core, root_zh, root_x = root % N_CORE, root // N_CORE % N_ZH, root // (N_CORE * N_ZH)
    has_keys = core == root_core
    got_values, gain = lax.optimization_barrier((send(values, dcore=1), gain.reshape(1, -1)))
    slabs = slabs_of(has_keys, keys, got_values)
    got = [slabs[0]] + [send(slabs[d], dx=d) for d in (1, 2, 3)]
    got, result = lax.optimization_barrier((got, beside(gain)))
    mine = pick(got, (x - root_x) % N_X)
    return over_rows(mine, zh, root_zh), has_keys, result


def from_row(mine, projected, o_weight):
    row = [mine] + [send(mine, dx=dx) for dx in (1, 3, 2)]
    other = [send(a, dcore=1) for a in row]
    row, projected, o_weight = lax.optimization_barrier((row, projected, o_weight))
    other, ready = lax.optimization_barrier((other, bring_in(projected, o_weight)))
    return row, other, ready


def bring_in(small, weight):
    chunks = 8
    size = weight.shape[0] // chunks

    def kernel(*refs):
        small_ref, weight_hbm, small_out, weight_out, sems = refs
        gets = [
            pltpu.make_async_copy(weight_hbm.at[pl.ds(i * size, size), :], weight_out.at[pl.ds(i * size, size), :], sems.at[i])
            for i in range(chunks)
        ]
        for get in gets:
            get.start()
        small_out[...] = small_ref[...]
        for get in gets:
            get.wait()

    return pl.pallas_call(
        kernel,
        in_specs=[VMEM, pl.BlockSpec(memory_space=pl.ANY)],
        out_specs=[VMEM] * 2,
        out_shape=[jax.ShapeDtypeStruct(a.shape, a.dtype) for a in (small, weight)],
        scratch_shapes=[pltpu.SemaphoreType.DMA((chunks,))],
        compiler_params=pltpu.CompilerParams(vmem_limit_bytes=BRING_GRANT * 2**20),
        cost_estimate=pl.CostEstimate(flops=0, bytes_accessed=2 * weight.size, transcendentals=0),
    )(small, weight)


def project(new_states, attn_gain, q_weight, k_weight, v_weight, prompt_len):
    step_count, samples, feature_dim = new_states.shape
    rows = step_count * samples
    q_width, head_dim = q_weight.shape[1], k_weight.shape[1]
    heads, half = q_width // head_dim, head_dim // 2
    depth = 512
    frequency = np.exp(-np.arange(half) * (np.log(500000.0) / half))
    angles = (prompt_len + np.repeat(np.arange(step_count), samples))[:, None] * frequency
    cosine = np.concatenate([np.cos(angles)] * 2, axis=1).astype(np.float32)
    sine = np.concatenate([-np.sin(angles), np.sin(angles)], axis=1).astype(np.float32)

    chunks = feature_dim // depth

    def kernel(x_hbm, gain_ref, cos_ref, sin_ref, wq_hbm, wk_hbm, wv_hbm, out_ref, x, wq, wk, wv, acc, sems):
        get_x = pltpu.make_async_copy(x_hbm, x, sems.at[0, chunks])
        get_x.start()
        gets = []
        for i in range(chunks):
            part = pl.ds(i * depth, depth)
            gets.append(
                [
                    pltpu.make_async_copy(hbm.at[part, :], ref.at[part, :], sems.at[j, i])
                    for j, (hbm, ref) in enumerate(((wq_hbm, wq), (wk_hbm, wk), (wv_hbm, wv)))
                ]
            )
            for get in gets[-1]:
                get.start()
        get_x.wait()
        squares = jnp.zeros((rows, 1), jnp.float32)
        for i in range(chunks):
            states = x[:, i * depth : (i + 1) * depth].astype(jnp.float32)
            squares += jnp.sum(states * states, axis=-1, keepdims=True)
        inv = lax.rsqrt(squares / feature_dim + epsilon)
        for i in range(chunks):
            part = slice(i * depth, (i + 1) * depth)
            states = x[:, part].astype(jnp.float32)
            gain = gain_ref[:, part].astype(jnp.float32)
            normed = (states * inv * gain).astype(jnp.bfloat16)
            at_column = 0
            for get, w in zip(gets[i], (wq, wk, wv)):
                get.wait()
                columns = slice(at_column, at_column + w.shape[1])
                product = jnp.dot(normed, w[part, :], preferred_element_type=jnp.float32)
                if i == 0:
                    acc[:, columns] = product
                else:
                    acc[:, columns] += product
                at_column += w.shape[1]

        def rotated(block):
            swapped = pltpu.roll(block, half, 1)
            return (block * cos_ref[...] + swapped * sin_ref[...]).astype(jnp.bfloat16)

        for head in range(heads):
            out_ref[head] = rotated(acc[:, head * head_dim : (head + 1) * head_dim])
        out_ref[heads] = rotated(acc[:, q_width : q_width + head_dim])
        out_ref[heads + 1] = acc[:, q_width + head_dim :].astype(jnp.bfloat16)

    anywhere = pl.BlockSpec(memory_space=pl.ANY)
    return pl.pallas_call(
        kernel,
        in_specs=[anywhere, VMEM, VMEM, VMEM, anywhere, anywhere, anywhere],
        out_specs=VMEM,
        out_shape=jax.ShapeDtypeStruct((heads + 2, rows, head_dim), jnp.bfloat16),
        scratch_shapes=[
            pltpu.VMEM((rows, feature_dim), jnp.bfloat16),
            pltpu.VMEM((feature_dim, q_width), jnp.bfloat16),
            pltpu.VMEM((feature_dim, head_dim), jnp.bfloat16),
            pltpu.VMEM((feature_dim, head_dim), jnp.bfloat16),
            pltpu.VMEM((rows, q_width + 2 * head_dim), jnp.float32),
            pltpu.SemaphoreType.DMA((3, chunks + 1)),
        ],
        compiler_params=pltpu.CompilerParams(vmem_limit_bytes=QKV_GRANT * 2**20),
        cost_estimate=pl.CostEstimate(
            flops=2 * rows * feature_dim * (q_width + 2 * head_dim),
            bytes_accessed=2 * feature_dim * (rows + q_width + 2 * head_dim),
            transcendentals=0,
        ),
    )(
        new_states.reshape(rows, feature_dim),
        attn_gain,
        cosine,
        sine,
        q_weight,
        k_weight,
        v_weight,
    )


def attend(projected, row, other, has_keys, o_weight, step_count):
    heads, rows, head_dim = projected.shape[0] - 2, *projected.shape[1:]
    samples = rows // step_count
    features = o_weight.shape[1]
    width = features // (N_Y * PARTS)
    scale = head_dim**-0.5
    pieces, positions = len(row), row[0].shape[0]

    def kernel(place_ref, qkv_ref, o_ref, *rest):
        row_refs, other_refs, rest = rest[:pieces], rest[pieces : 2 * pieces], rest[2 * pieces :]
        out_refs, (keys, values, scores) = rest[: PARTS * N_Y], rest[PARTS * N_Y :]

        @pl.when(place_ref[1] == 1)
        def _():
            for p in range(pieces):
                keys[p], values[p] = row_refs[p][...], other_refs[p][...]

        @pl.when(place_ref[1] == 0)
        def _():
            for p in range(pieces):
                keys[p], values[p] = other_refs[p][...], row_refs[p][...]

        step_of = lax.broadcasted_iota(jnp.int32, (rows, 1), 0) // samples
        keys_of = [jnp.concatenate([qkv_ref[heads, u * samples : (u + 1) * samples]] * step_count, axis=0).astype(jnp.float32) for u in range(step_count)]
        values_of = [jnp.concatenate([qkv_ref[heads + 1, u * samples : (u + 1) * samples]] * step_count, axis=0).astype(jnp.float32) for u in range(step_count)]
        q_all = qkv_ref[:heads].reshape(heads * rows, head_dim)
        row_max = None
        for i in range(pieces):
            s = lax.dot_general(q_all, keys[i], (((1,), (1,)), ((), ())), preferred_element_type=jnp.float32)
            scores[i] = s
            top = jnp.max(s, axis=1, keepdims=True)
            row_max = top if row_max is None else jnp.maximum(row_max, top)
        row_sum = jnp.zeros((heads * rows, 1), jnp.float32)
        weighted = jnp.zeros((heads * rows, head_dim), jnp.float32)
        for i in range(pieces):
            e = jnp.exp2((scores[i] - row_max) * (scale * np.log2(np.e)))
            row_sum += jnp.sum(e, axis=1, keepdims=True)
            weighted += jnp.dot(e.astype(jnp.bfloat16), values[i], preferred_element_type=jnp.float32)
        row_max = row_max * scale
        attended = []
        for head in range(heads):
            part = slice(head * rows, (head + 1) * rows)
            q32 = qkv_ref[head].astype(jnp.float32)
            joint_max, own = row_max[part], []
            for u in range(step_count):
                s = jnp.sum(q32 * keys_of[u], axis=1, keepdims=True) * scale
                s = jnp.where(step_of >= u, s, -1e30)
                joint_max = jnp.maximum(joint_max, s)
                own.append(s)
            rescale = jnp.exp(row_max[part] - joint_max)
            denominator = row_sum[part] * rescale
            numerator = weighted[part] * rescale
            for u in range(step_count):
                e = jnp.where(step_of >= u, jnp.exp(own[u] - joint_max), 0.0)
                denominator += e
                numerator += e.astype(jnp.bfloat16).astype(jnp.float32) * values_of[u]
            attended.append((numerator / denominator).astype(jnp.bfloat16))
        attended = jnp.concatenate(attended, axis=1)
        for i in range(PARTS * N_Y):
            column = lax.rem(place_ref[0] + i % N_Y, N_Y) * (PARTS * width) + i // N_Y * width
            o_block = o_ref[:, pl.ds(pl.multiple_of(column, width), width)]
            out_refs[i][...] = jnp.dot(attended, o_block, preferred_element_type=jnp.float32).astype(jnp.bfloat16)

    place = jnp.stack([lax.axis_index("tp") % N_Y, has_keys.astype(jnp.int32)])
    vmem = pl.BlockSpec(memory_space=pltpu.VMEM)
    return pl.pallas_call(
        kernel,
        in_specs=[pl.BlockSpec(memory_space=pltpu.SMEM)] + [vmem] * (2 + 2 * pieces),
        out_specs=[vmem] * (PARTS * N_Y),
        out_shape=[jax.ShapeDtypeStruct((rows, width), jnp.bfloat16)] * (PARTS * N_Y),
        scratch_shapes=[
            pltpu.VMEM((pieces, positions, head_dim), jnp.bfloat16),
            pltpu.VMEM((pieces, positions, head_dim), jnp.bfloat16),
            pltpu.VMEM((pieces, heads * rows, positions), jnp.float32),
        ],
        compiler_params=pltpu.CompilerParams(vmem_limit_bytes=24 * 2**20),
        cost_estimate=pl.CostEstimate(
            flops=2 * rows * features * o_weight.shape[0] + 8 * heads * rows * pieces * positions * head_dim,
            bytes_accessed=2 * o_weight.size + 4 * pieces * row[0].size,
            transcendentals=0,
        ),
    )(place, projected, o_weight, *row, *other)


def add_up(parts):
    got = [[blocks[0]] + [send(blocks[d], dy=d) for d in (1, 2, 3)] for blocks in parts]
    along_y = [sum(a.astype(jnp.float32) for a in terms).astype(jnp.bfloat16) for terms in got]
    across = [send(a, dzl=1) for a in along_y]
    blocks = [
        (a.astype(jnp.float32) + b.astype(jnp.float32)).astype(jnp.bfloat16)
        for a, b in zip(along_y, across)
    ]
    return [[block] + [send(block, dy=d) for d in (1, 2, 3)] for block in blocks]


def lay_out(parts):
    rows, width = parts[0][0].shape

    def kernel(y_ref, *rest):
        ins, out = rest[: PARTS * N_Y], rest[PARTS * N_Y]
        for i in range(PARTS * N_Y):
            column = lax.rem(y_ref[0] + N_Y - i % N_Y, N_Y) * (PARTS * width) + i // N_Y * width
            out[:, pl.ds(pl.multiple_of(column, width), width)] = ins[i][...]

    vmem = pl.BlockSpec(memory_space=pltpu.VMEM)
    return pl.pallas_call(
        kernel,
        in_specs=[pl.BlockSpec(memory_space=pltpu.SMEM)] + [vmem] * (PARTS * N_Y),
        out_specs=vmem,
        out_shape=jax.ShapeDtypeStruct((rows, PARTS * N_Y * width), parts[0][0].dtype),
        compiler_params=pltpu.CompilerParams(vmem_limit_bytes=8 * 2**20),
    )(lax.axis_index("tp").reshape(1) % N_Y, *[block for blocks in parts for block in blocks])


def on_device(
    new_states,
    attn_gain,
    q_weight,
    k_weight,
    v_weight,
    o_weight,
    prompt_keys,
    prompt_values,
    owner_index,
):
    step_count, samples, _ = new_states.shape
    project_all = lambda gain: project(
        new_states, gain, q_weight, k_weight, v_weight, prompt_keys.shape[1]
    )
    piece, has_keys, projected = broadcast(
        prompt_keys[0], prompt_values[0], owner_index[0], attn_gain, project_all
    )
    row, other, (projected, o_near) = from_row(piece, projected, o_weight)
    partial_blocks = attend(projected, row, other, has_keys, o_near, step_count)
    summed = lay_out(add_up([partial_blocks[i * N_Y : (i + 1) * N_Y] for i in range(PARTS)]))
    return summed.reshape(step_count, samples, o_weight.shape[1])


def solution(mesh):
    placed = (
        P(None, "inst", None),
        P(),
        P(None, "tp"),
        P(None, "tp"),
        P(None, "tp"),
        P("tp", None),
        P("inst", None, "tp"),
        P("inst", None, "tp"),
        P(),
    )
    return jax.shard_map(
        on_device, mesh=mesh, in_specs=placed, out_specs=P(None, "inst", None), check_vma=False
    )
```

```python
import jax
import jax.numpy as jnp
import numpy as np
from jax import lax
from jax.experimental import pallas as pl
from jax.experimental.pallas import tpu as pltpu
from jax.sharding import PartitionSpec as P

HD = 128
PARTS = 2
ATTEND_GRANT = 24
COPIES = 8
QKV_GRANT = 56
ROW_ORDER = (2, 3, 1)


epsilon = 1e-05

AXES = ("inst", "tp")
N_X, N_ZH, N_CORE = 4, 4, 2
N_ZL, N_Y = 2, 4


def at(x, zh, core, zl, y):
    inst = (x % N_X * N_ZH + zh % N_ZH) * N_CORE + core % N_CORE
    return inst * (N_ZL * N_Y) + zl % N_ZL * N_Y + y % N_Y


def send(block, dx=0, dzh=0, dcore=0, dzl=0, dy=0, only=lambda x, zh, core: True):
    pairs = [
        (at(x, zh, core, zl, y), at(x + dx, zh + dzh, core + dcore, zl + dzl, y + dy))
        for x in range(N_X)
        for zh in range(N_ZH)
        for core in range(N_CORE)
        for zl in range(N_ZL)
        for y in range(N_Y)
        if only(x, zh, core)
    ]
    return lax.ppermute(block, AXES, pairs)


VMEM = pl.BlockSpec(memory_space=pltpu.VMEM)
SMEM = pl.BlockSpec(memory_space=pltpu.SMEM)


def pick(pieces, index):
    def kernel(index_ref, *refs):
        for d, ref in enumerate(refs[:-1]):

            @pl.when(index_ref[0] == d)
            def _():
                refs[-1][...] = ref[...]

    return pl.pallas_call(
        kernel,
        in_specs=[SMEM] + [VMEM] * len(pieces),
        out_specs=VMEM,
        out_shape=jax.ShapeDtypeStruct(pieces[0].shape, pieces[0].dtype),
        compiler_params=pltpu.CompilerParams(vmem_limit_bytes=4 * 2**20),
    )(index.reshape(1), *pieces)


def slabs_of(first, keys, values):
    size, width = keys.shape[0] // N_X, keys.shape[1]

    def kernel(first_ref, keys_ref, values_ref, *slabs):
        for want, ref in ((1, keys_ref), (0, values_ref)):

            @pl.when(first_ref[0] == want)
            def _():
                for d in range(N_X):
                    slabs[d][...] = ref[d * size : (d + 1) * size]

    return pl.pallas_call(
        kernel,
        in_specs=[SMEM, VMEM, VMEM],
        out_specs=[VMEM] * N_X,
        out_shape=[jax.ShapeDtypeStruct((size, width), keys.dtype)] * N_X,
        compiler_params=pltpu.CompilerParams(vmem_limit_bytes=4 * 2**20),
    )(first.astype(jnp.int32).reshape(1), keys, values)


def over_rows(piece, zh, root_zh):
    def branch(from_zh):
        def run(piece):
            only = lambda x, zh, core: zh == from_zh
            got = {d: send(piece, dzh=d, only=only) for d in ROW_ORDER}
            place = sum(((from_zh + d) % N_ZH == zh) * (i + 1) for i, d in enumerate(ROW_ORDER))
            return pick([piece] + [got[d] for d in ROW_ORDER], place)

        return run

    return lax.switch(root_zh, [branch(a) for a in range(N_ZH)], piece)


def broadcast(keys, values, root, beside):
    me = lax.axis_index("inst")
    core, zh, x = me % N_CORE, me // N_CORE % N_ZH, me // (N_CORE * N_ZH)
    root_core, root_zh, root_x = root % N_CORE, root // N_CORE % N_ZH, root // (N_CORE * N_ZH)
    has_keys = core == root_core
    slabs = slabs_of(has_keys, keys, send(values, dcore=1))
    got = [slabs[0]] + [send(slabs[d], dx=d) for d in (1, 2, 3)]
    got, result = lax.optimization_barrier((got, beside()))
    mine = pick(got, (x - root_x) % N_X)
    return over_rows(mine, zh, root_zh), has_keys, result


def from_row(mine):
    row = [mine] + [send(mine, dx=dx) for dx in (1, 3, 2)]
    return row, [send(a, dcore=1) for a in row]


def project(new_states, attn_gain, q_weight, k_weight, v_weight, prompt_len):
    step_count, samples, feature_dim = new_states.shape
    rows = step_count * samples
    q_width, head_dim = q_weight.shape[1], k_weight.shape[1]
    heads, half = q_width // head_dim, head_dim // 2
    depth = 512
    frequency = np.exp(-np.arange(half) * (np.log(500000.0) / half))
    angles = (prompt_len + np.repeat(np.arange(step_count), samples))[:, None] * frequency
    cosine = np.concatenate([np.cos(angles)] * 2, axis=1).astype(np.float32)
    sine = np.concatenate([-np.sin(angles), np.sin(angles)], axis=1).astype(np.float32)

    chunks = feature_dim // depth

    def kernel(x_hbm, gain_ref, cos_ref, sin_ref, wq_hbm, wk_hbm, wv_hbm, out_ref, x, wq, wk, wv, acc, sems):
        get_x = pltpu.make_async_copy(x_hbm, x, sems.at[0, chunks])
        get_x.start()
        gets = []
        for i in range(chunks):
            part = pl.ds(i * depth, depth)
            gets.append(
                [
                    pltpu.make_async_copy(hbm.at[part, :], ref.at[part, :], sems.at[j, i])
                    for j, (hbm, ref) in enumerate(((wq_hbm, wq), (wk_hbm, wk), (wv_hbm, wv)))
                ]
            )
            for get in gets[-1]:
                get.start()
        get_x.wait()
        squares = jnp.zeros((rows, 1), jnp.float32)
        for i in range(chunks):
            states = x[:, i * depth : (i + 1) * depth].astype(jnp.float32)
            squares += jnp.sum(states * states, axis=-1, keepdims=True)
        inv = lax.rsqrt(squares / feature_dim + epsilon)
        for i in range(chunks):
            part = slice(i * depth, (i + 1) * depth)
            gain = gain_ref[i * depth // 128 : (i + 1) * depth // 128].astype(jnp.float32)
            normed = jnp.concatenate(
                [
                    (x[:, c * 128 : (c + 1) * 128].astype(jnp.float32) * inv * gain[c - i * depth // 128]).astype(jnp.bfloat16)
                    for c in range(i * depth // 128, (i + 1) * depth // 128)
                ],
                axis=1,
            )
            at_column = 0
            for get, w in zip(gets[i], (wq, wk, wv)):
                get.wait()
                columns = slice(at_column, at_column + w.shape[1])
                product = jnp.dot(normed, w[part, :], preferred_element_type=jnp.float32)
                if i == 0:
                    acc[:, columns] = product
                else:
                    acc[:, columns] += product
                at_column += w.shape[1]

        def rotated(block):
            swapped = pltpu.roll(block, half, 1)
            return (block * cos_ref[...] + swapped * sin_ref[...]).astype(jnp.bfloat16)

        for head in range(heads):
            out_ref[head] = rotated(acc[:, head * head_dim : (head + 1) * head_dim])
        out_ref[heads] = rotated(acc[:, q_width : q_width + head_dim])
        out_ref[heads + 1] = acc[:, q_width + head_dim :].astype(jnp.bfloat16)

    anywhere = pl.BlockSpec(memory_space=pl.ANY)
    return pl.pallas_call(
        kernel,
        in_specs=[anywhere, VMEM, VMEM, VMEM, anywhere, anywhere, anywhere],
        out_specs=VMEM,
        out_shape=pltpu.VMEM((heads + 2, rows, head_dim), jnp.bfloat16),
        scratch_shapes=[
            pltpu.VMEM((rows, feature_dim), jnp.bfloat16),
            pltpu.VMEM((feature_dim, q_width), jnp.bfloat16),
            pltpu.VMEM((feature_dim, head_dim), jnp.bfloat16),
            pltpu.VMEM((feature_dim, head_dim), jnp.bfloat16),
            pltpu.VMEM((rows, q_width + 2 * head_dim), jnp.float32),
            pltpu.SemaphoreType.DMA((3, chunks + 1)),
        ],
        compiler_params=pltpu.CompilerParams(vmem_limit_bytes=QKV_GRANT * 2**20),
        cost_estimate=pl.CostEstimate(
            flops=2 * rows * feature_dim * (q_width + 2 * head_dim),
            bytes_accessed=2 * feature_dim * (rows + q_width + 2 * head_dim),
            transcendentals=0,
        ),
    )(
        new_states.reshape(rows, feature_dim),
        attn_gain.reshape(feature_dim // 128, 128),
        cosine,
        sine,
        q_weight,
        k_weight,
        v_weight,
    )


def attend(projected, row, other, has_keys, o_weight, step_count):
    heads, rows, head_dim = projected.shape[0] - 2, *projected.shape[1:]
    samples = rows // step_count
    features = o_weight.shape[1]
    width = features // (N_Y * PARTS)
    scale = head_dim**-0.5
    pieces, positions = len(row), row[0].shape[0]

    def kernel(place_ref, qkv_ref, o_hbm, *rest):
        row_refs, other_refs, rest = rest[:pieces], rest[pieces : 2 * pieces], rest[2 * pieces :]
        out_refs, (keys, values, scores, o_near, sems) = rest[: PARTS * N_Y], rest[PARTS * N_Y :]
        parts = [pl.ds(i * o_near.shape[0] // COPIES, o_near.shape[0] // COPIES) for i in range(COPIES)]
        gets = [
            pltpu.make_async_copy(o_hbm.at[part, :], o_near.at[part, :], sems.at[i])
            for i, part in enumerate(parts)
        ]
        for get in gets:
            get.start()

        @pl.when(place_ref[1] == 1)
        def _():
            for p in range(pieces):
                keys[p], values[p] = row_refs[p][...], other_refs[p][...]

        @pl.when(place_ref[1] == 0)
        def _():
            for p in range(pieces):
                keys[p], values[p] = other_refs[p][...], row_refs[p][...]

        step_of = lax.broadcasted_iota(jnp.int32, (rows, 1), 0) // samples
        keys_of = [jnp.concatenate([qkv_ref[heads, u * samples : (u + 1) * samples]] * step_count, axis=0).astype(jnp.float32) for u in range(step_count)]
        values_of = [jnp.concatenate([qkv_ref[heads + 1, u * samples : (u + 1) * samples]] * step_count, axis=0).astype(jnp.float32) for u in range(step_count)]
        q_all = qkv_ref[:heads].reshape(heads * rows, head_dim)
        row_max = None
        for i in range(pieces):
            s = lax.dot_general(q_all, keys[i], (((1,), (1,)), ((), ())), preferred_element_type=jnp.float32)
            scores[i] = s
            top = jnp.max(s, axis=1, keepdims=True)
            row_max = top if row_max is None else jnp.maximum(row_max, top)
        row_sum = jnp.zeros((heads * rows, 1), jnp.float32)
        weighted = jnp.zeros((heads * rows, head_dim), jnp.float32)
        for i in range(pieces):
            e = jnp.exp2((scores[i] - row_max) * (scale * np.log2(np.e)))
            row_sum += jnp.sum(e, axis=1, keepdims=True)
            weighted += jnp.dot(e.astype(jnp.bfloat16), values[i], preferred_element_type=jnp.float32)
        row_max = row_max * scale
        attended = []
        for head in range(heads):
            part = slice(head * rows, (head + 1) * rows)
            q32 = qkv_ref[head].astype(jnp.float32)
            joint_max, own = row_max[part], []
            for u in range(step_count):
                s = jnp.sum(q32 * keys_of[u], axis=1, keepdims=True) * scale
                s = jnp.where(step_of >= u, s, -1e30)
                joint_max = jnp.maximum(joint_max, s)
                own.append(s)
            rescale = jnp.exp(row_max[part] - joint_max)
            denominator = row_sum[part] * rescale
            numerator = weighted[part] * rescale
            for u in range(step_count):
                e = jnp.where(step_of >= u, jnp.exp(own[u] - joint_max), 0.0)
                denominator += e
                numerator += e.astype(jnp.bfloat16).astype(jnp.float32) * values_of[u]
            attended.append((numerator / denominator).astype(jnp.bfloat16))
        attended = jnp.concatenate(attended, axis=1)
        for get in gets:
            get.wait()
        for i in range(PARTS * N_Y):
            column = lax.rem(place_ref[0] + i % N_Y, N_Y) * (PARTS * width) + i // N_Y * width
            o_block = o_near[:, pl.ds(pl.multiple_of(column, width), width)]
            out_refs[i][...] = jnp.dot(attended, o_block, preferred_element_type=jnp.float32).astype(jnp.bfloat16)

    place = jnp.stack([lax.axis_index("tp") % N_Y, has_keys.astype(jnp.int32)])
    vmem = pl.BlockSpec(memory_space=pltpu.VMEM)
    return pl.pallas_call(
        kernel,
        in_specs=[pl.BlockSpec(memory_space=pltpu.SMEM)] + [vmem, pl.BlockSpec(memory_space=pltpu.HBM)] + [vmem] * (2 * pieces),
        out_specs=[vmem] * (PARTS * N_Y),
        out_shape=[jax.ShapeDtypeStruct((rows, width), jnp.bfloat16)] * (PARTS * N_Y),
        scratch_shapes=[
            pltpu.VMEM((pieces, positions, head_dim), jnp.bfloat16),
            pltpu.VMEM((pieces, positions, head_dim), jnp.bfloat16),
            pltpu.VMEM((pieces, heads * rows, positions), jnp.float32),
            pltpu.VMEM(o_weight.shape, jnp.bfloat16),
            pltpu.SemaphoreType.DMA((COPIES,)),
        ],
        compiler_params=pltpu.CompilerParams(vmem_limit_bytes=ATTEND_GRANT * 2**20),
        cost_estimate=pl.CostEstimate(
            flops=2 * rows * features * o_weight.shape[0] + 8 * heads * rows * pieces * positions * head_dim,
            bytes_accessed=2 * o_weight.size + 4 * pieces * row[0].size,
            transcendentals=0,
        ),
    )(
        place,
        pltpu.with_memory_space_constraint(projected, pltpu.VMEM),
        pltpu.with_memory_space_constraint(o_weight, pltpu.HBM),
        *row,
        *other,
    )


def add_up(parts):
    got = [[blocks[0]] + [send(blocks[d], dy=d) for d in (1, 2, 3)] for blocks in parts]
    along_y = [sum(a.astype(jnp.float32) for a in terms).astype(jnp.bfloat16) for terms in got]
    across = [send(a, dzl=1) for a in along_y]
    blocks = [
        (a.astype(jnp.float32) + b.astype(jnp.float32)).astype(jnp.bfloat16)
        for a, b in zip(along_y, across)
    ]
    return [[block] + [send(block, dy=d) for d in (1, 2, 3)] for block in blocks]


def lay_out(parts):
    rows, width = parts[0][0].shape

    def kernel(y_ref, *rest):
        ins, out = rest[: PARTS * N_Y], rest[PARTS * N_Y]
        for i in range(PARTS * N_Y):
            column = lax.rem(y_ref[0] + N_Y - i % N_Y, N_Y) * (PARTS * width) + i // N_Y * width
            out[:, pl.ds(pl.multiple_of(column, width), width)] = ins[i][...]

    vmem = pl.BlockSpec(memory_space=pltpu.VMEM)
    return pl.pallas_call(
        kernel,
        in_specs=[pl.BlockSpec(memory_space=pltpu.SMEM)] + [vmem] * (PARTS * N_Y),
        out_specs=vmem,
        out_shape=jax.ShapeDtypeStruct((rows, PARTS * N_Y * width), parts[0][0].dtype),
        compiler_params=pltpu.CompilerParams(vmem_limit_bytes=8 * 2**20),
    )(lax.axis_index("tp").reshape(1) % N_Y, *[block for blocks in parts for block in blocks])


def on_device(
    new_states,
    attn_gain,
    q_weight,
    k_weight,
    v_weight,
    o_weight,
    prompt_keys,
    prompt_values,
    owner_index,
):
    step_count, samples, _ = new_states.shape
    project_all = lambda: project(
        new_states, attn_gain, q_weight, k_weight, v_weight, prompt_keys.shape[1]
    )
    piece, has_keys, projected = broadcast(
        prompt_keys[0], prompt_values[0], owner_index[0], project_all
    )
    row, other = from_row(piece)
    partial_blocks = attend(projected, row, other, has_keys, o_weight, step_count)
    summed = lay_out(add_up([partial_blocks[i * N_Y : (i + 1) * N_Y] for i in range(PARTS)]))
    return summed.reshape(step_count, samples, o_weight.shape[1])


def solution(mesh):
    placed = (
        P(None, "inst", None),
        P(),
        P(None, "tp"),
        P(None, "tp"),
        P(None, "tp"),
        P("tp", None),
        P("inst", None, "tp"),
        P("inst", None, "tp"),
        P(),
    )
    return jax.shard_map(
        on_device, mesh=mesh, in_specs=placed, out_specs=P(None, "inst", None), check_vma=False
    )
```

```python
import jax
import jax.numpy as jnp
import numpy as np
from jax import lax
from jax.experimental import pallas as pl
from jax.experimental.pallas import tpu as pltpu
from jax.sharding import PartitionSpec as P

HD = 128
PARTS = 2
ATTEND_GRANT = 24
COPIES = 8
QKV_GRANT = 56
ROW_ORDER = (2, 3, 1)


epsilon = 1e-05

AXES = ("inst", "tp")
N_X, N_ZH, N_CORE = 4, 4, 2
N_ZL, N_Y = 2, 4


def at(x, zh, core, zl, y):
    inst = (x % N_X * N_ZH + zh % N_ZH) * N_CORE + core % N_CORE
    return inst * (N_ZL * N_Y) + zl % N_ZL * N_Y + y % N_Y


def send(block, dx=0, dzh=0, dcore=0, dzl=0, dy=0, only=lambda x, zh, core: True):
    pairs = [
        (at(x, zh, core, zl, y), at(x + dx, zh + dzh, core + dcore, zl + dzl, y + dy))
        for x in range(N_X)
        for zh in range(N_ZH)
        for core in range(N_CORE)
        for zl in range(N_ZL)
        for y in range(N_Y)
        if only(x, zh, core)
    ]
    return lax.ppermute(block, AXES, pairs)


VMEM = pl.BlockSpec(memory_space=pltpu.VMEM)
SMEM = pl.BlockSpec(memory_space=pltpu.SMEM)


def pick(pieces, index):
    def kernel(index_ref, *refs):
        for d, ref in enumerate(refs[:-1]):

            @pl.when(index_ref[0] == d)
            def _():
                refs[-1][...] = ref[...]

    return pl.pallas_call(
        kernel,
        in_specs=[SMEM] + [VMEM] * len(pieces),
        out_specs=VMEM,
        out_shape=jax.ShapeDtypeStruct(pieces[0].shape, pieces[0].dtype),
        compiler_params=pltpu.CompilerParams(vmem_limit_bytes=4 * 2**20),
    )(index.reshape(1), *pieces)


def bring_in(array):
    size = array.shape[0] // COPIES

    def kernel(hbm, out, sems):
        parts = [pl.ds(i * size, size) for i in range(COPIES)]
        gets = [
            pltpu.make_async_copy(hbm.at[part, :], out.at[part, :], sems.at[i])
            for i, part in enumerate(parts)
        ]
        for get in gets:
            get.start()
        for get in gets:
            get.wait()

    return pl.pallas_call(
        kernel,
        in_specs=[pl.BlockSpec(memory_space=pltpu.HBM)],
        out_specs=VMEM,
        out_shape=pltpu.VMEM(array.shape, array.dtype),
        scratch_shapes=[pltpu.SemaphoreType.DMA((COPIES,))],
        compiler_params=pltpu.CompilerParams(vmem_limit_bytes=4 * 2**20),
    )(pltpu.with_memory_space_constraint(array, pltpu.HBM))


def slabs_of(first, keys, values):
    size, width = keys.shape[0] // N_X, keys.shape[1]

    def kernel(first_ref, keys_ref, values_ref, *slabs):
        for want, ref in ((1, keys_ref), (0, values_ref)):

            @pl.when(first_ref[0] == want)
            def _():
                for d in range(N_X):
                    slabs[d][...] = ref[d * size : (d + 1) * size]

    return pl.pallas_call(
        kernel,
        in_specs=[SMEM, VMEM, VMEM],
        out_specs=[VMEM] * N_X,
        out_shape=[jax.ShapeDtypeStruct((size, width), keys.dtype)] * N_X,
        compiler_params=pltpu.CompilerParams(vmem_limit_bytes=4 * 2**20),
    )(first.astype(jnp.int32).reshape(1), keys, values)


def over_rows(piece, zh, root_zh):
    def branch(from_zh):
        def run(piece):
            only = lambda x, zh, core: zh == from_zh
            got = {d: send(piece, dzh=d, only=only) for d in ROW_ORDER}
            place = sum(((from_zh + d) % N_ZH == zh) * (i + 1) for i, d in enumerate(ROW_ORDER))
            return pick([piece] + [got[d] for d in ROW_ORDER], place)

        return run

    return lax.switch(root_zh, [branch(a) for a in range(N_ZH)], piece)


def broadcast(keys, values, root, beside):
    me = lax.axis_index("inst")
    core, zh, x = me % N_CORE, me // N_CORE % N_ZH, me // (N_CORE * N_ZH)
    root_core, root_zh, root_x = root % N_CORE, root // N_CORE % N_ZH, root // (N_CORE * N_ZH)
    has_keys = core == root_core
    got_values = send(values, dcore=1)
    slabs = slabs_of(has_keys, bring_in(keys), got_values)
    got = [slabs[0]] + [send(slabs[d], dx=d) for d in (1, 2, 3)]
    got, result = lax.optimization_barrier((got, beside()))
    mine = pick(got, (x - root_x) % N_X)
    return over_rows(mine, zh, root_zh), has_keys, result


def from_row(mine):
    row = [mine] + [send(mine, dx=dx) for dx in (1, 3, 2)]
    return row, [send(a, dcore=1) for a in row]


def project(new_states, attn_gain, q_weight, k_weight, v_weight, prompt_len):
    step_count, samples, feature_dim = new_states.shape
    rows = step_count * samples
    q_width, head_dim = q_weight.shape[1], k_weight.shape[1]
    heads, half = q_width // head_dim, head_dim // 2
    depth = 512
    frequency = np.exp(-np.arange(half) * (np.log(500000.0) / half))
    angles = (prompt_len + np.repeat(np.arange(step_count), samples))[:, None] * frequency
    cosine = np.concatenate([np.cos(angles)] * 2, axis=1).astype(np.float32)
    sine = np.concatenate([-np.sin(angles), np.sin(angles)], axis=1).astype(np.float32)

    chunks = feature_dim // depth

    def kernel(x_hbm, gain_ref, cos_ref, sin_ref, wq_hbm, wk_hbm, wv_hbm, out_ref, x, wq, wk, wv, acc, sems):
        get_x = pltpu.make_async_copy(x_hbm, x, sems.at[0, chunks])
        get_x.start()
        gets = []
        for i in range(chunks):
            part = pl.ds(i * depth, depth)
            gets.append(
                [
                    pltpu.make_async_copy(hbm.at[part, :], ref.at[part, :], sems.at[j, i])
                    for j, (hbm, ref) in enumerate(((wq_hbm, wq), (wk_hbm, wk), (wv_hbm, wv)))
                ]
            )
            for get in gets[-1]:
                get.start()
        get_x.wait()
        squares = jnp.zeros((rows, 1), jnp.float32)
        for i in range(chunks):
            states = x[:, i * depth : (i + 1) * depth].astype(jnp.float32)
            squares += jnp.sum(states * states, axis=-1, keepdims=True)
        inv = lax.rsqrt(squares / feature_dim + epsilon)
        for i in range(chunks):
            part = slice(i * depth, (i + 1) * depth)
            gain = gain_ref[i * depth // 128 : (i + 1) * depth // 128].astype(jnp.float32)
            normed = jnp.concatenate(
                [
                    (x[:, c * 128 : (c + 1) * 128].astype(jnp.float32) * inv * gain[c - i * depth // 128]).astype(jnp.bfloat16)
                    for c in range(i * depth // 128, (i + 1) * depth // 128)
                ],
                axis=1,
            )
            at_column = 0
            for get, w in zip(gets[i], (wq, wk, wv)):
                get.wait()
                columns = slice(at_column, at_column + w.shape[1])
                product = jnp.dot(normed, w[part, :], preferred_element_type=jnp.float32)
                if i == 0:
                    acc[:, columns] = product
                else:
                    acc[:, columns] += product
                at_column += w.shape[1]

        def rotated(block):
            swapped = pltpu.roll(block, half, 1)
            return (block * cos_ref[...] + swapped * sin_ref[...]).astype(jnp.bfloat16)

        for head in range(heads):
            out_ref[head] = rotated(acc[:, head * head_dim : (head + 1) * head_dim])
        out_ref[heads] = rotated(acc[:, q_width : q_width + head_dim])
        out_ref[heads + 1] = acc[:, q_width + head_dim :].astype(jnp.bfloat16)

    anywhere = pl.BlockSpec(memory_space=pl.ANY)
    return pl.pallas_call(
        kernel,
        in_specs=[anywhere, VMEM, VMEM, VMEM, anywhere, anywhere, anywhere],
        out_specs=VMEM,
        out_shape=pltpu.VMEM((heads + 2, rows, head_dim), jnp.bfloat16),
        scratch_shapes=[
            pltpu.VMEM((rows, feature_dim), jnp.bfloat16),
            pltpu.VMEM((feature_dim, q_width), jnp.bfloat16),
            pltpu.VMEM((feature_dim, head_dim), jnp.bfloat16),
            pltpu.VMEM((feature_dim, head_dim), jnp.bfloat16),
            pltpu.VMEM((rows, q_width + 2 * head_dim), jnp.float32),
            pltpu.SemaphoreType.DMA((3, chunks + 1)),
        ],
        compiler_params=pltpu.CompilerParams(vmem_limit_bytes=QKV_GRANT * 2**20),
        cost_estimate=pl.CostEstimate(
            flops=2 * rows * feature_dim * (q_width + 2 * head_dim),
            bytes_accessed=2 * feature_dim * (rows + q_width + 2 * head_dim),
            transcendentals=0,
        ),
    )(
        new_states.reshape(rows, feature_dim),
        attn_gain.reshape(feature_dim // 128, 128),
        cosine,
        sine,
        q_weight,
        k_weight,
        v_weight,
    )


def attend(projected, row, other, has_keys, o_weight, step_count):
    heads, rows, head_dim = projected.shape[0] - 2, *projected.shape[1:]
    samples = rows // step_count
    features = o_weight.shape[1]
    width = features // (N_Y * PARTS)
    scale = head_dim**-0.5
    pieces, positions = len(row), row[0].shape[0]

    def kernel(place_ref, qkv_ref, o_hbm, *rest):
        row_refs, other_refs, rest = rest[:pieces], rest[pieces : 2 * pieces], rest[2 * pieces :]
        out_refs, (keys, values, scores, o_near, sems) = rest[: PARTS * N_Y], rest[PARTS * N_Y :]
        parts = [pl.ds(i * o_near.shape[0] // COPIES, o_near.shape[0] // COPIES) for i in range(COPIES)]
        gets = [
            pltpu.make_async_copy(o_hbm.at[part, :], o_near.at[part, :], sems.at[i])
            for i, part in enumerate(parts)
        ]
        for get in gets:
            get.start()

        @pl.when(place_ref[1] == 1)
        def _():
            for p in range(pieces):
                keys[p], values[p] = row_refs[p][...], other_refs[p][...]

        @pl.when(place_ref[1] == 0)
        def _():
            for p in range(pieces):
                keys[p], values[p] = other_refs[p][...], row_refs[p][...]

        step_of = lax.broadcasted_iota(jnp.int32, (rows, 1), 0) // samples
        keys_of = [jnp.concatenate([qkv_ref[heads, u * samples : (u + 1) * samples]] * step_count, axis=0).astype(jnp.float32) for u in range(step_count)]
        values_of = [jnp.concatenate([qkv_ref[heads + 1, u * samples : (u + 1) * samples]] * step_count, axis=0).astype(jnp.float32) for u in range(step_count)]
        q_all = qkv_ref[:heads].reshape(heads * rows, head_dim)
        row_max = None
        for i in range(pieces):
            s = lax.dot_general(q_all, keys[i], (((1,), (1,)), ((), ())), preferred_element_type=jnp.float32)
            scores[i] = s
            top = jnp.max(s, axis=1, keepdims=True)
            row_max = top if row_max is None else jnp.maximum(row_max, top)
        row_sum = jnp.zeros((heads * rows, 1), jnp.float32)
        weighted = jnp.zeros((heads * rows, head_dim), jnp.float32)
        for i in range(pieces):
            e = jnp.exp2((scores[i] - row_max) * (scale * np.log2(np.e)))
            row_sum += jnp.sum(e, axis=1, keepdims=True)
            weighted += jnp.dot(e.astype(jnp.bfloat16), values[i], preferred_element_type=jnp.float32)
        row_max = row_max * scale
        attended = []
        for head in range(heads):
            part = slice(head * rows, (head + 1) * rows)
            q32 = qkv_ref[head].astype(jnp.float32)
            joint_max, own = row_max[part], []
            for u in range(step_count):
                s = jnp.sum(q32 * keys_of[u], axis=1, keepdims=True) * scale
                s = jnp.where(step_of >= u, s, -1e30)
                joint_max = jnp.maximum(joint_max, s)
                own.append(s)
            rescale = jnp.exp(row_max[part] - joint_max)
            denominator = row_sum[part] * rescale
            numerator = weighted[part] * rescale
            for u in range(step_count):
                e = jnp.where(step_of >= u, jnp.exp(own[u] - joint_max), 0.0)
                denominator += e
                numerator += e.astype(jnp.bfloat16).astype(jnp.float32) * values_of[u]
            attended.append((numerator / denominator).astype(jnp.bfloat16))
        attended = jnp.concatenate(attended, axis=1)
        for get in gets:
            get.wait()
        for i in range(PARTS * N_Y):
            column = lax.rem(place_ref[0] + i % N_Y, N_Y) * (PARTS * width) + i // N_Y * width
            o_block = o_near[:, pl.ds(pl.multiple_of(column, width), width)]
            out_refs[i][...] = jnp.dot(attended, o_block, preferred_element_type=jnp.float32).astype(jnp.bfloat16)

    place = jnp.stack([lax.axis_index("tp") % N_Y, has_keys.astype(jnp.int32)])
    vmem = pl.BlockSpec(memory_space=pltpu.VMEM)
    return pl.pallas_call(
        kernel,
        in_specs=[pl.BlockSpec(memory_space=pltpu.SMEM)] + [vmem, pl.BlockSpec(memory_space=pltpu.HBM)] + [vmem] * (2 * pieces),
        out_specs=[vmem] * (PARTS * N_Y),
        out_shape=[jax.ShapeDtypeStruct((rows, width), jnp.bfloat16)] * (PARTS * N_Y),
        scratch_shapes=[
            pltpu.VMEM((pieces, positions, head_dim), jnp.bfloat16),
            pltpu.VMEM((pieces, positions, head_dim), jnp.bfloat16),
            pltpu.VMEM((pieces, heads * rows, positions), jnp.float32),
            pltpu.VMEM(o_weight.shape, jnp.bfloat16),
            pltpu.SemaphoreType.DMA((COPIES,)),
        ],
        compiler_params=pltpu.CompilerParams(vmem_limit_bytes=ATTEND_GRANT * 2**20),
        cost_estimate=pl.CostEstimate(
            flops=2 * rows * features * o_weight.shape[0] + 8 * heads * rows * pieces * positions * head_dim,
            bytes_accessed=2 * o_weight.size + 4 * pieces * row[0].size,
            transcendentals=0,
        ),
    )(
        place,
        pltpu.with_memory_space_constraint(projected, pltpu.VMEM),
        pltpu.with_memory_space_constraint(o_weight, pltpu.HBM),
        *row,
        *other,
    )


def add_up(parts):
    got = [[blocks[0]] + [send(blocks[d], dy=d) for d in (1, 2, 3)] for blocks in parts]
    along_y = [sum(a.astype(jnp.float32) for a in terms).astype(jnp.bfloat16) for terms in got]
    across = [send(a, dzl=1) for a in along_y]
    blocks = [
        (a.astype(jnp.float32) + b.astype(jnp.float32)).astype(jnp.bfloat16)
        for a, b in zip(along_y, across)
    ]
    return [[block] + [send(block, dy=d) for d in (1, 2, 3)] for block in blocks]


def lay_out(parts):
    rows, width = parts[0][0].shape

    def kernel(y_ref, *rest):
        ins, out = rest[: PARTS * N_Y], rest[PARTS * N_Y]
        for i in range(PARTS * N_Y):
            column = lax.rem(y_ref[0] + N_Y - i % N_Y, N_Y) * (PARTS * width) + i // N_Y * width
            out[:, pl.ds(pl.multiple_of(column, width), width)] = ins[i][...]

    vmem = pl.BlockSpec(memory_space=pltpu.VMEM)
    return pl.pallas_call(
        kernel,
        in_specs=[pl.BlockSpec(memory_space=pltpu.SMEM)] + [vmem] * (PARTS * N_Y),
        out_specs=vmem,
        out_shape=jax.ShapeDtypeStruct((rows, PARTS * N_Y * width), parts[0][0].dtype),
        compiler_params=pltpu.CompilerParams(vmem_limit_bytes=8 * 2**20),
    )(lax.axis_index("tp").reshape(1) % N_Y, *[block for blocks in parts for block in blocks])


def on_device(
    new_states,
    attn_gain,
    q_weight,
    k_weight,
    v_weight,
    o_weight,
    prompt_keys,
    prompt_values,
    owner_index,
):
    step_count, samples, _ = new_states.shape
    project_all = lambda: project(
        new_states, attn_gain, q_weight, k_weight, v_weight, prompt_keys.shape[1]
    )
    piece, has_keys, projected = broadcast(
        prompt_keys[0], prompt_values[0], owner_index[0], project_all
    )
    row, other = from_row(piece)
    partial_blocks = attend(projected, row, other, has_keys, o_weight, step_count)
    summed = lay_out(add_up([partial_blocks[i * N_Y : (i + 1) * N_Y] for i in range(PARTS)]))
    return summed.reshape(step_count, samples, o_weight.shape[1])


def solution(mesh):
    placed = (
        P(None, "inst", None),
        P(),
        P(None, "tp"),
        P(None, "tp"),
        P(None, "tp"),
        P("tp", None),
        P("inst", None, "tp"),
        P("inst", None, "tp"),
        P(),
    )
    return jax.shard_map(
        on_device, mesh=mesh, in_specs=placed, out_specs=P(None, "inst", None), check_vma=False
    )
```

```python
import jax
import jax.numpy as jnp
import numpy as np
from jax import lax
from jax.experimental import pallas as pl
from jax.experimental.pallas import tpu as pltpu
from jax.sharding import PartitionSpec as P

HD = 128
PARTS = 2
ATTEND_GRANT = 24
COPIES = 8
QKV_GRANT = 56
ROW_ORDER = (2, 3, 1)


epsilon = 1e-05

AXES = ("inst", "tp")
N_X, N_ZH, N_CORE = 4, 4, 2
N_ZL, N_Y = 2, 4


def at(x, zh, core, zl, y):
    inst = (x % N_X * N_ZH + zh % N_ZH) * N_CORE + core % N_CORE
    return inst * (N_ZL * N_Y) + zl % N_ZL * N_Y + y % N_Y


def send(block, dx=0, dzh=0, dcore=0, dzl=0, dy=0, only=lambda x, zh, core: True):
    pairs = [
        (at(x, zh, core, zl, y), at(x + dx, zh + dzh, core + dcore, zl + dzl, y + dy))
        for x in range(N_X)
        for zh in range(N_ZH)
        for core in range(N_CORE)
        for zl in range(N_ZL)
        for y in range(N_Y)
        if only(x, zh, core)
    ]
    return lax.ppermute(block, AXES, pairs)


VMEM = pl.BlockSpec(memory_space=pltpu.VMEM)
SMEM = pl.BlockSpec(memory_space=pltpu.SMEM)


def pick(pieces, index):
    def kernel(index_ref, *refs):
        for d, ref in enumerate(refs[:-1]):

            @pl.when(index_ref[0] == d)
            def _():
                refs[-1][...] = ref[...]

    return pl.pallas_call(
        kernel,
        in_specs=[SMEM] + [VMEM] * len(pieces),
        out_specs=VMEM,
        out_shape=jax.ShapeDtypeStruct(pieces[0].shape, pieces[0].dtype),
        compiler_params=pltpu.CompilerParams(vmem_limit_bytes=4 * 2**20),
    )(index.reshape(1), *pieces)


def bring_in(array):
    size = array.shape[0] // COPIES

    def kernel(hbm, out, sems):
        parts = [pl.ds(i * size, size) for i in range(COPIES)]
        gets = [
            pltpu.make_async_copy(hbm.at[part, :], out.at[part, :], sems.at[i])
            for i, part in enumerate(parts)
        ]
        for get in gets:
            get.start()
        for get in gets:
            get.wait()

    return pl.pallas_call(
        kernel,
        in_specs=[pl.BlockSpec(memory_space=pltpu.HBM)],
        out_specs=VMEM,
        out_shape=pltpu.VMEM(array.shape, array.dtype),
        scratch_shapes=[pltpu.SemaphoreType.DMA((COPIES,))],
        compiler_params=pltpu.CompilerParams(vmem_limit_bytes=4 * 2**20),
    )(pltpu.with_memory_space_constraint(array, pltpu.HBM))


def slabs_of(first, keys, values):
    size, width = keys.shape[0] // N_X, keys.shape[1]

    def kernel(first_ref, keys_ref, values_ref, *slabs):
        for want, ref in ((1, keys_ref), (0, values_ref)):

            @pl.when(first_ref[0] == want)
            def _():
                for d in range(N_X):
                    slabs[d][...] = ref[d * size : (d + 1) * size]

    return pl.pallas_call(
        kernel,
        in_specs=[SMEM, VMEM, VMEM],
        out_specs=[VMEM] * N_X,
        out_shape=[jax.ShapeDtypeStruct((size, width), keys.dtype)] * N_X,
        compiler_params=pltpu.CompilerParams(vmem_limit_bytes=4 * 2**20),
    )(first.astype(jnp.int32).reshape(1), keys, values)


def over_rows(piece, zh, root_zh):
    def branch(from_zh):
        def run(piece):
            only = lambda x, zh, core: zh == from_zh
            got = {d: send(piece, dzh=d, only=only) for d in ROW_ORDER}
            place = sum(((from_zh + d) % N_ZH == zh) * (i + 1) for i, d in enumerate(ROW_ORDER))
            return pick([piece] + [got[d] for d in ROW_ORDER], place)

        return run

    return lax.switch(root_zh, [branch(a) for a in range(N_ZH)], piece)


def broadcast(keys, values, root, beside):
    me = lax.axis_index("inst")
    core, zh, x = me % N_CORE, me // N_CORE % N_ZH, me // (N_CORE * N_ZH)
    root_core, root_zh, root_x = root % N_CORE, root // N_CORE % N_ZH, root // (N_CORE * N_ZH)
    has_keys = core == root_core
    got_values = send(values, dcore=1)
    slabs = slabs_of(has_keys, bring_in(keys), got_values)
    got = [slabs[0]] + [send(slabs[d], dx=d) for d in (1, 2, 3)]
    got, result = lax.optimization_barrier((got, beside()))
    mine = pick(got, (x - root_x) % N_X)
    return over_rows(mine, zh, root_zh), has_keys, result


def from_row(mine):
    row = [mine] + [send(mine, dx=dx) for dx in (1, 3, 2)]
    return row, [send(a, dcore=1) for a in row]


def project(new_states, attn_gain, q_weight, k_weight, v_weight, prompt_len):
    step_count, samples, feature_dim = new_states.shape
    rows = step_count * samples
    q_width, head_dim = q_weight.shape[1], k_weight.shape[1]
    heads, half = q_width // head_dim, head_dim // 2
    depth = 512
    frequency = np.exp(-np.arange(half) * (np.log(500000.0) / half))
    angles = (prompt_len + np.repeat(np.arange(step_count), samples))[:, None] * frequency
    cosine = np.concatenate([np.cos(angles)] * 2, axis=1).astype(np.float32)
    sine = np.concatenate([-np.sin(angles), np.sin(angles)], axis=1).astype(np.float32)

    chunks = feature_dim // depth

    def kernel(x_hbm, gain_ref, cos_ref, sin_ref, wq_hbm, wk_hbm, wv_hbm, out_ref, x, wq, wk, wv, acc, sems):
        get_x = pltpu.make_async_copy(x_hbm, x, sems.at[0, chunks])
        get_x.start()
        gets = []
        for i in range(chunks):
            part = pl.ds(i * depth, depth)
            gets.append(
                [
                    pltpu.make_async_copy(hbm.at[part, :], ref.at[part, :], sems.at[j, i])
                    for j, (hbm, ref) in enumerate(((wq_hbm, wq), (wk_hbm, wk), (wv_hbm, wv)))
                ]
            )
            for get in gets[-1]:
                get.start()
        get_x.wait()
        squares = jnp.zeros((rows, 1), jnp.float32)
        for i in range(chunks):
            states = x[:, i * depth : (i + 1) * depth].astype(jnp.float32)
            squares += jnp.sum(states * states, axis=-1, keepdims=True)
        inv = lax.rsqrt(squares / feature_dim + epsilon)
        gain = gain_ref[...].astype(jnp.float32)
        for i in range(chunks):
            part = slice(i * depth, (i + 1) * depth)
            normed = jnp.concatenate(
                [
                    (x[:, c * 128 : (c + 1) * 128].astype(jnp.float32) * inv * gain[c : c + 1]).astype(jnp.bfloat16)
                    for c in range(i * depth // 128, (i + 1) * depth // 128)
                ],
                axis=1,
            )
            at_column = 0
            for get, w in zip(gets[i], (wq, wk, wv)):
                get.wait()
                columns = slice(at_column, at_column + w.shape[1])
                product = jnp.dot(normed, w[part, :], preferred_element_type=jnp.float32)
                if i == 0:
                    acc[:, columns] = product
                else:
                    acc[:, columns] += product
                at_column += w.shape[1]

        def rotated(block):
            swapped = pltpu.roll(block, half, 1)
            return (block * cos_ref[...] + swapped * sin_ref[...]).astype(jnp.bfloat16)

        for head in range(heads):
            out_ref[head] = rotated(acc[:, head * head_dim : (head + 1) * head_dim])
        out_ref[heads] = rotated(acc[:, q_width : q_width + head_dim])
        out_ref[heads + 1] = acc[:, q_width + head_dim :].astype(jnp.bfloat16)

    anywhere = pl.BlockSpec(memory_space=pl.ANY)
    return pl.pallas_call(
        kernel,
        in_specs=[anywhere, VMEM, VMEM, VMEM, anywhere, anywhere, anywhere],
        out_specs=VMEM,
        out_shape=pltpu.VMEM((heads + 2, rows, head_dim), jnp.bfloat16),
        scratch_shapes=[
            pltpu.VMEM((rows, feature_dim), jnp.bfloat16),
            pltpu.VMEM((feature_dim, q_width), jnp.bfloat16),
            pltpu.VMEM((feature_dim, head_dim), jnp.bfloat16),
            pltpu.VMEM((feature_dim, head_dim), jnp.bfloat16),
            pltpu.VMEM((rows, q_width + 2 * head_dim), jnp.float32),
            pltpu.SemaphoreType.DMA((3, chunks + 1)),
        ],
        compiler_params=pltpu.CompilerParams(vmem_limit_bytes=QKV_GRANT * 2**20),
        cost_estimate=pl.CostEstimate(
            flops=2 * rows * feature_dim * (q_width + 2 * head_dim),
            bytes_accessed=2 * feature_dim * (rows + q_width + 2 * head_dim),
            transcendentals=0,
        ),
    )(
        new_states.reshape(rows, feature_dim),
        attn_gain.reshape(feature_dim // 128, 128),
        cosine,
        sine,
        q_weight,
        k_weight,
        v_weight,
    )


def attend(projected, row, other, has_keys, o_weight, step_count):
    heads, rows, head_dim = projected.shape[0] - 2, *projected.shape[1:]
    samples = rows // step_count
    features = o_weight.shape[1]
    width = features // (N_Y * PARTS)
    scale = head_dim**-0.5
    pieces, positions = len(row), row[0].shape[0]

    def kernel(place_ref, qkv_ref, o_hbm, *rest):
        row_refs, other_refs, rest = rest[:pieces], rest[pieces : 2 * pieces], rest[2 * pieces :]
        out_refs, (keys, values, scores, o_near, sems) = rest[: PARTS * N_Y], rest[PARTS * N_Y :]
        parts = [pl.ds(i * o_near.shape[0] // COPIES, o_near.shape[0] // COPIES) for i in range(COPIES)]
        gets = [
            pltpu.make_async_copy(o_hbm.at[part, :], o_near.at[part, :], sems.at[i])
            for i, part in enumerate(parts)
        ]
        for get in gets:
            get.start()

        @pl.when(place_ref[1] == 1)
        def _():
            for p in range(pieces):
                keys[p], values[p] = row_refs[p][...], other_refs[p][...]

        @pl.when(place_ref[1] == 0)
        def _():
            for p in range(pieces):
                keys[p], values[p] = other_refs[p][...], row_refs[p][...]

        step_of = lax.broadcasted_iota(jnp.int32, (rows, 1), 0) // samples
        keys_of = [jnp.concatenate([qkv_ref[heads, u * samples : (u + 1) * samples]] * step_count, axis=0).astype(jnp.float32) for u in range(step_count)]
        values_of = [jnp.concatenate([qkv_ref[heads + 1, u * samples : (u + 1) * samples]] * step_count, axis=0).astype(jnp.float32) for u in range(step_count)]
        q_all = qkv_ref[:heads].reshape(heads * rows, head_dim)
        row_max = None
        for i in range(pieces):
            s = lax.dot_general(q_all, keys[i], (((1,), (1,)), ((), ())), preferred_element_type=jnp.float32)
            scores[i] = s
            top = jnp.max(s, axis=1, keepdims=True)
            row_max = top if row_max is None else jnp.maximum(row_max, top)
        row_sum = jnp.zeros((heads * rows, 1), jnp.float32)
        weighted = jnp.zeros((heads * rows, head_dim), jnp.float32)
        for i in range(pieces):
            e = jnp.exp2((scores[i] - row_max) * (scale * np.log2(np.e)))
            row_sum += jnp.sum(e, axis=1, keepdims=True)
            weighted += jnp.dot(e.astype(jnp.bfloat16), values[i], preferred_element_type=jnp.float32)
        row_max = row_max * scale
        attended = []
        for head in range(heads):
            part = slice(head * rows, (head + 1) * rows)
            q32 = qkv_ref[head].astype(jnp.float32)
            joint_max, own = row_max[part], []
            for u in range(step_count):
                s = jnp.sum(q32 * keys_of[u], axis=1, keepdims=True) * scale
                s = jnp.where(step_of >= u, s, -1e30)
                joint_max = jnp.maximum(joint_max, s)
                own.append(s)
            rescale = jnp.exp(row_max[part] - joint_max)
            denominator = row_sum[part] * rescale
            numerator = weighted[part] * rescale
            for u in range(step_count):
                e = jnp.where(step_of >= u, jnp.exp(own[u] - joint_max), 0.0)
                denominator += e
                numerator += e.astype(jnp.bfloat16).astype(jnp.float32) * values_of[u]
            attended.append((numerator / denominator).astype(jnp.bfloat16))
        attended = jnp.concatenate(attended, axis=1)
        for get in gets:
            get.wait()
        for i in range(PARTS * N_Y):
            column = lax.rem(place_ref[0] + i % N_Y, N_Y) * (PARTS * width) + i // N_Y * width
            o_block = o_near[:, pl.ds(pl.multiple_of(column, width), width)]
            out_refs[i][...] = jnp.dot(attended, o_block, preferred_element_type=jnp.float32).astype(jnp.bfloat16)

    place = jnp.stack([lax.axis_index("tp") % N_Y, has_keys.astype(jnp.int32)])
    vmem = pl.BlockSpec(memory_space=pltpu.VMEM)
    return pl.pallas_call(
        kernel,
        in_specs=[pl.BlockSpec(memory_space=pltpu.SMEM)] + [vmem, pl.BlockSpec(memory_space=pltpu.HBM)] + [vmem] * (2 * pieces),
        out_specs=[vmem] * (PARTS * N_Y),
        out_shape=[jax.ShapeDtypeStruct((rows, width), jnp.bfloat16)] * (PARTS * N_Y),
        scratch_shapes=[
            pltpu.VMEM((pieces, positions, head_dim), jnp.bfloat16),
            pltpu.VMEM((pieces, positions, head_dim), jnp.bfloat16),
            pltpu.VMEM((pieces, heads * rows, positions), jnp.float32),
            pltpu.VMEM(o_weight.shape, jnp.bfloat16),
            pltpu.SemaphoreType.DMA((COPIES,)),
        ],
        compiler_params=pltpu.CompilerParams(vmem_limit_bytes=ATTEND_GRANT * 2**20),
        cost_estimate=pl.CostEstimate(
            flops=2 * rows * features * o_weight.shape[0] + 8 * heads * rows * pieces * positions * head_dim,
            bytes_accessed=2 * o_weight.size + 4 * pieces * row[0].size,
            transcendentals=0,
        ),
    )(
        place,
        pltpu.with_memory_space_constraint(projected, pltpu.VMEM),
        pltpu.with_memory_space_constraint(o_weight, pltpu.HBM),
        *row,
        *other,
    )


def add_up(parts):
    got = [[blocks[0]] + [send(blocks[d], dy=d) for d in (1, 2, 3)] for blocks in parts]
    along_y = [sum(a.astype(jnp.float32) for a in terms).astype(jnp.bfloat16) for terms in got]
    across = [send(a, dzl=1) for a in along_y]
    blocks = [
        (a.astype(jnp.float32) + b.astype(jnp.float32)).astype(jnp.bfloat16)
        for a, b in zip(along_y, across)
    ]
    return [[block] + [send(block, dy=d) for d in (1, 2, 3)] for block in blocks]


def lay_out(parts):
    rows, width = parts[0][0].shape

    def kernel(y_ref, *rest):
        ins, out = rest[: PARTS * N_Y], rest[PARTS * N_Y]
        for i in range(PARTS * N_Y):
            column = lax.rem(y_ref[0] + N_Y - i % N_Y, N_Y) * (PARTS * width) + i // N_Y * width
            out[:, pl.ds(pl.multiple_of(column, width), width)] = ins[i][...]

    vmem = pl.BlockSpec(memory_space=pltpu.VMEM)
    return pl.pallas_call(
        kernel,
        in_specs=[pl.BlockSpec(memory_space=pltpu.SMEM)] + [vmem] * (PARTS * N_Y),
        out_specs=vmem,
        out_shape=jax.ShapeDtypeStruct((rows, PARTS * N_Y * width), parts[0][0].dtype),
        compiler_params=pltpu.CompilerParams(vmem_limit_bytes=8 * 2**20),
    )(lax.axis_index("tp").reshape(1) % N_Y, *[block for blocks in parts for block in blocks])


def on_device(
    new_states,
    attn_gain,
    q_weight,
    k_weight,
    v_weight,
    o_weight,
    prompt_keys,
    prompt_values,
    owner_index,
):
    step_count, samples, _ = new_states.shape
    project_all = lambda: project(
        new_states, attn_gain, q_weight, k_weight, v_weight, prompt_keys.shape[1]
    )
    piece, has_keys, projected = broadcast(
        prompt_keys[0], prompt_values[0], owner_index[0], project_all
    )
    row, other = from_row(piece)
    partial_blocks = attend(projected, row, other, has_keys, o_weight, step_count)
    summed = lay_out(add_up([partial_blocks[i * N_Y : (i + 1) * N_Y] for i in range(PARTS)]))
    return summed.reshape(step_count, samples, o_weight.shape[1])


def solution(mesh):
    placed = (
        P(None, "inst", None),
        P(),
        P(None, "tp"),
        P(None, "tp"),
        P(None, "tp"),
        P("tp", None),
        P("inst", None, "tp"),
        P("inst", None, "tp"),
        P(),
    )
    return jax.shard_map(
        on_device, mesh=mesh, in_specs=placed, out_specs=P(None, "inst", None), check_vma=False
    )
```
